32 devices in a mesh: dp: 2 (over x), seq: 4 (over z), enc: 4 (over y, core).
Axes of the slice: x: 2, y: 2, z: 4, core: 2. Of those that a mesh axis runs over, the one named last changes fastest.
Arguments:
- queries: bfloat16 [8, 512, 512], P(('dp', 'enc'), 'seq'), may hold values from -12 to 12
- cotangent: bfloat16 [8, 512, 512], P(('dp', 'enc'), 'seq'), may hold values from -12 to 12
- key_pool: bfloat16 [2, 4, 8, 128, 512], P('dp', 'seq', None, None, 'enc'), may hold values from -12 to 12
- value_pool: bfloat16 [2, 4, 8, 128, 512], P('dp', 'seq', None, None, 'enc'), may hold values from -6 to 6
- counts: int32 [8, 8], P('dp', 'seq'), may hold values from 0 to 4
- neighbour_ids: int32 [8, 8, 4], P('dp', 'seq'), may hold values from 0 to 7, all different within a row
- rel_bias: float32 [4, 191], P('enc'), may hold values from -3 to 3
Outputs:
- context: bfloat16 [8, 512, 512], P(('dp', 'enc'), 'seq')
- query_grad: bfloat16 [8, 512, 512], P(('dp', 'enc'), 'seq')
- key_grad: bfloat16 [2, 4, 8, 128, 512], P('dp', 'seq', None, None, 'enc')
- value_grad: bfloat16 [2, 4, 8, 128, 512], P('dp', 'seq', None, None, 'enc')
- bias_grad: float32 [4, 191], P('enc')
The draws below stay inside these ranges and needn't reach their ends.
Inputs may be any that keep to these rules, and one draw needn't show every extreme that they name: Only the first counts[c] ids of a block are used. `neighbour_ids`: the 4 ids of one block are distinct.
All inputs are finite; a program needn't handle non-finite values.
Results may differ from the reference program's by a relative error of at most 0.0085.
Values may be sent and summed in bfloat16 or wider, within the bound.
A program may use at most 64 MiB of HBM per device.

```python
import math
import jax
import jax.numpy as jnp
from jax import lax

HEAD_DIM = 128
BLOCK_LEN = 64
PASSAGE = 128
NEIGHBOURS = 4
TOK_DEV = 128
POOL = 8
HEADS = 4
SEQS = 8
LENGTH = 512
BLOCKS_SEQ = 8
REL = 191
DATA_GROUPS = 2
SPANS = 4
N_DP = 2
N_SEQ = 4
N_ENC = 4


def draw_queries(key, part):
    base = jax.random.truncated_normal(jax.random.fold_in(key, 1), -6.0, 6.0, (SEQS, LENGTH, HEADS, HEAD_DIM), jnp.float32)
    return base.reshape(SEQS, LENGTH, HEADS * HEAD_DIM).astype(jnp.bfloat16)


def draw_key_pool(key, part):
    base = jax.random.truncated_normal(jax.random.fold_in(key, 2), -6.0, 6.0, (DATA_GROUPS, SPANS, POOL, PASSAGE, HEADS, HEAD_DIM), jnp.float32)
    return base.reshape(DATA_GROUPS, SPANS, POOL, PASSAGE, HEADS * HEAD_DIM).astype(jnp.bfloat16)


def set_ends(values, stream_key, least, high):
    dims = values.shape
    index_at = [jax.random.randint(jax.random.fold_in(stream_key, axis), (), 0, dims[axis]) for axis in range(len(dims))]
    values = values.at[tuple(index_at)].set(least)
    longest = dims.index(max(dims))
    index_at[longest] = (index_at[longest] + 1) % dims[longest]
    return values.at[tuple(index_at)].set(high)


def block_levels(own_key, extent, split, low, top_value):
    level, own = 1.0, jax.random.fold_in(own_key, 6)
    for axis_at, blocks in split:
        steps = jnp.exp(jax.random.uniform(jax.random.fold_in(own, axis_at), (blocks,), jnp.float32, low / len(split), top_value / len(split)))
        level = level * jnp.repeat(steps, extent[axis_at] // blocks).reshape([-1 if axis == axis_at else 1 for axis in range(len(extent))])
    return level


def picks_of(rng, rows, amount, top, lift):
    sequence = jax.random.permutation(jax.random.fold_in(rng, 1), amount)
    favour = sequence
    for power in range(3):
        favour = favour * favour // amount
    favour = favour * lift // amount
    tickets = jax.random.randint(jax.random.fold_in(rng, 2), (rows, amount), 0, 4096) + favour
    holders = jax.random.permutation(jax.random.fold_in(rng, 3), rows)[jnp.arange(amount) % rows]
    tickets = jnp.where(jnp.arange(rows)[:, None] == holders[None, :], 1 << 14, tickets)
    priority = tickets * amount + jnp.arange(amount)
    return lax.top_k(priority.astype(jnp.int32), top)[1].astype(jnp.int32)


def noise(own_key, dims, scale, limit, cuts=(), kind=jnp.bfloat16):
    result = jax.random.normal(own_key, dims, jnp.float32) * scale
    if len(cuts) > 0:
        result = block_levels(own_key, dims, cuts, -0.22, 0.18) * result
    return jnp.clip(result, min=-limit, max=limit).astype(kind)


def setup_inputs(seed: int = 0) -> dict:
    streams_of = jax.random.split(jax.random.key(seed), 8)
    queries = draw_queries(jax.random.fold_in(streams_of[7], 71), 0)
    cotangent = noise(streams_of[1], (SEQS, LENGTH, HEADS * HEAD_DIM), 2.0, 12.0, ((0, 8), (1, 4)))
    key_pool = draw_key_pool(jax.random.fold_in(streams_of[7], 71), 0)
    value_pool = noise(streams_of[3], (DATA_GROUPS, SPANS, POOL, PASSAGE, HEADS * HEAD_DIM), 1.0, 6.0, ((0, 2), (1, 4), (4, 4)))
    counts = set_ends(jax.random.randint(streams_of[4], (SEQS, BLOCKS_SEQ), 0, NEIGHBOURS + 1), jax.random.fold_in(streams_of[4], 1), 0, NEIGHBOURS).astype(jnp.int32)
    neighbour_ids = picks_of(streams_of[5], SEQS * BLOCKS_SEQ, POOL, NEIGHBOURS, 0).reshape((SEQS, BLOCKS_SEQ, NEIGHBOURS))
    rel_bias = noise(streams_of[6], (HEADS, REL), 0.5, 3.0, ((0, 4),), jnp.float32)
    return dict(queries=queries, cotangent=cotangent, key_pool=key_pool, value_pool=value_pool, counts=counts, neighbour_ids=neighbour_ids, rel_bias=rel_bias)


NEG_FILL = -1e+30

def one_item(pieces):
    query_rows, grad_rows, pool_keys, pool_values, block_counts, block_ids, bias_line = pieces
    score_scale = 1.0 / math.sqrt(HEAD_DIM)
    offsets = (jnp.arange(PASSAGE)[None, :] - jnp.arange(BLOCK_LEN)[:, None] + BLOCK_LEN - 1).astype(jnp.int32)
    row_bias = bias_line[offsets]
    keys_sel = pool_keys[block_ids].astype(jnp.float32)
    values_sel = pool_values[block_ids].astype(jnp.float32)
    query_f = query_rows.astype(jnp.float32)
    grad_f = grad_rows.astype(jnp.float32)
    scores = jnp.einsum('cqd,cjtd->cqjt', query_f, keys_sel) * score_scale + row_bias[None, :, None, :]
    usable = (jnp.arange(NEIGHBOURS)[None, :] < block_counts[:, None])[:, None, :, None]
    row_top = lax.optimization_barrier(jnp.max(jnp.where(usable, scores, NEG_FILL), axis=(2, 3), keepdims=True))
    raised = jnp.where(usable, jnp.exp(scores - row_top), 0.0)
    no_keys = (block_counts == 0).astype(jnp.float32)[:, None, None, None]
    weights = raised / (lax.optimization_barrier(jnp.sum(raised, axis=(2, 3), keepdims=True)) + no_keys)
    weights_low = lax.optimization_barrier(weights.astype(jnp.bfloat16)).astype(jnp.float32)
    context = jnp.einsum('cqjt,cjtd->cqd', weights_low, values_sel).astype(jnp.bfloat16)
    grad_weights = jnp.einsum('cqd,cjtd->cqjt', grad_f, values_sel)
    row_delta = lax.optimization_barrier(jnp.sum(weights * grad_weights, axis=(2, 3), keepdims=True))
    grad_scores = weights * (grad_weights - row_delta)
    scores_low = lax.optimization_barrier(grad_scores.astype(jnp.bfloat16)).astype(jnp.float32)
    query_grad = (score_scale * jnp.einsum('cqjt,cjtd->cqd', scores_low, keys_sel)).astype(jnp.bfloat16)
    selector = (block_ids[:, :, None] == jnp.arange(POOL).astype(jnp.int32)[None, None, :]).astype(jnp.float32)
    key_slots = jnp.einsum('cqjt,cqd->cjtd', scores_low, query_f)
    key_grad = (score_scale * jnp.einsum('cjn,cjtd->ntd', selector, key_slots, precision=lax.Precision.HIGHEST)).astype(jnp.bfloat16)
    value_slots = jnp.einsum('cqjt,cqd->cjtd', weights_low, grad_f)
    value_grad = jnp.einsum('cjn,cjtd->ntd', selector, value_slots, precision=lax.Precision.HIGHEST).astype(jnp.bfloat16)
    bias_part = jax.ops.segment_sum(lax.optimization_barrier(jnp.sum(grad_scores, axis=(0, 2))).reshape(-1), offsets.reshape(-1), num_segments=REL)
    return (context, query_grad, key_grad, value_grad, bias_part)

def reference(queries, cotangent, key_pool, value_pool, counts, neighbour_ids, rel_bias):
    blocks_dev = TOK_DEV // BLOCK_LEN
    group_blocks = N_ENC * blocks_dev
    groups = N_DP * N_SEQ

    def token_heads(source):
        shaped = source.reshape(N_DP, N_ENC, N_SEQ, blocks_dev, BLOCK_LEN, HEADS, HEAD_DIM)
        return shaped.transpose(0, 2, 5, 1, 3, 4, 6).reshape(groups * HEADS, group_blocks, BLOCK_LEN, HEAD_DIM)

    def pool_heads(source):
        shaped = source.reshape(N_DP, N_SEQ, POOL, PASSAGE, HEADS, HEAD_DIM)
        return shaped.transpose(0, 1, 4, 2, 3, 5).reshape(groups * HEADS, POOL, PASSAGE, HEAD_DIM)
    count_rows = counts.reshape(N_DP, N_ENC, N_SEQ, blocks_dev).transpose(0, 2, 1, 3).reshape(groups, group_blocks)
    count_rows = jnp.repeat(count_rows, HEADS, axis=0)
    id_rows = neighbour_ids.reshape(N_DP, N_ENC, N_SEQ, blocks_dev, NEIGHBOURS).transpose(0, 2, 1, 3, 4)
    id_rows = jnp.repeat(id_rows.reshape(groups, group_blocks, NEIGHBOURS), HEADS, axis=0)
    bias_rows = jnp.tile(rel_bias, (groups, 1))
    results = lax.map(one_item, (token_heads(queries), token_heads(cotangent), pool_heads(key_pool), pool_heads(value_pool), count_rows, id_rows, bias_rows))

    def back_tokens(source):
        shaped = source.reshape(N_DP, N_SEQ, HEADS, N_ENC, blocks_dev, BLOCK_LEN, HEAD_DIM)
        return shaped.transpose(0, 3, 1, 4, 5, 2, 6).reshape(SEQS, LENGTH, HEADS * HEAD_DIM)

    def back_pool(source):
        shaped = source.reshape(N_DP, N_SEQ, HEADS, POOL, PASSAGE, HEAD_DIM)
        return shaped.transpose(0, 1, 3, 4, 2, 5).reshape(N_DP, N_SEQ, POOL, PASSAGE, HEADS * HEAD_DIM)
    bias_grad = results[4].reshape(groups, HEADS, REL).sum(axis=0)
    return (back_tokens(results[0]), back_tokens(results[1]), back_pool(results[2]), back_pool(results[3]), bias_grad)
```

```python
import functools
import math

import jax
import jax.numpy as jnp
from jax import lax
from jax.experimental import pallas as pl
from jax.experimental.pallas import tpu as pltpu
from jax.sharding import PartitionSpec as P

HEAD_DIM = 128
BLOCK_LEN = 64
PASSAGE = 128
ROWS = 128
WIDE = 256

NEG_FILL = -1e30
SCALE = 1.0 / math.sqrt(HEAD_DIM)
LOG2E = math.log2(math.e)
F32 = jnp.float32
BF16 = jnp.bfloat16
MESH = pl.DeviceIdType.MESH


def each(low, high, body):
    if high - low <= 8:
        for step in range(low, high):
            body(step)
    else:

        def one(step, carry):
            body(step)
            return carry

        lax.fori_loop(low, high, one, 0)


def span(index):
    if isinstance(index, int):
        return pl.ds(index * ROWS, ROWS)
    return pl.ds(pl.multiple_of(index * ROWS, ROWS), ROWS)


def dot(left, right, left_dim, right_dim):
    return lax.dot_general(
        left, right, (((left_dim,), (right_dim,)), ((), ())), preferred_element_type=F32
    )


def spread_bias(line):
    rows = jnp.broadcast_to(line * LOG2E, (8, WIDE))
    sub = lax.broadcasted_iota(jnp.int32, (8, WIDE), 0)
    rows = pltpu.roll(rows, WIDE - (BLOCK_LEN - 1), 1)
    for bit in (1, 2, 4):
        rows = jnp.where((sub & bit) != 0, pltpu.roll(rows, bit, 1), rows)
    groups = [rows] + [pltpu.roll(rows, 8 * k, 1) for k in range(1, BLOCK_LEN // 8)]
    block = jnp.concatenate([group[:, :PASSAGE] for group in groups], axis=0)
    return jnp.concatenate([block, block], axis=0).T


def fold_bias(total):
    turned = total.T
    block = turned[:BLOCK_LEN] + turned[BLOCK_LEN:]
    block = jnp.concatenate([block, jnp.zeros((BLOCK_LEN, WIDE - PASSAGE), F32)], axis=1)
    for half in (32, 16, 8):
        block = pltpu.roll(block[:half], half, 1) + block[half : 2 * half]
    sub = lax.broadcasted_iota(jnp.int32, (8, WIDE), 0)
    for bit in (4, 2, 1):
        block = jnp.where((sub & bit) == 0, pltpu.roll(block, bit, 1), block)
    return jnp.sum(block, axis=0, keepdims=True)


def kernel(
    n_dp, n_seq, n_enc, pool, slots,
    q_hbm, g_hbm, k_hbm, v_hbm, count_hbm, id_hbm, bias_hbm,
    context_out, query_out, key_out, value_out, bias_out,
    q_buf, g_buf, k_buf, v_buf, k_turn, v_turn, counts, ids, line, wide_line, bias_map,
    s_buf, d_buf, w_all, ds_all, bias_sum, c_buf, dq_buf, dk_buf, dv_buf, parts, bias_row,
    load_sem, own_sem, store_sem,
    q_send, q_recv, g_send, g_recv, c_send, c_recv, dq_send, dq_recv, b_send, b_recv,
):
    dp, seq, enc = lax.axis_index("dp"), lax.axis_index("seq"), lax.axis_index("enc")
    total = n_dp * n_seq
    flat = dp * n_seq + seq
    table = line.shape[1]

    def to_peer(step):
        return lax.rem(enc + step, n_enc)

    def from_peer(step):
        return lax.rem(enc + (n_enc - step), n_enc)

    def group_at(place):
        return (place // n_seq, lax.rem(place, n_seq), enc)

    def other(step):
        return lax.rem(flat + step, total)

    barrier = pltpu.get_barrier_semaphore()

    def greet(step):
        pl.semaphore_signal(barrier, inc=1, device_id=(dp, seq, to_peer(step)), device_id_type=MESH)

    def greet_group(step):
        pl.semaphore_signal(barrier, inc=1, device_id=group_at(other(step)), device_id_type=MESH)

    each(1, n_enc, greet)
    each(1, total, greet_group)

    loads = [
        (bias_hbm, line),
        (count_hbm, counts),
        (id_hbm, ids),
        (k_hbm, k_buf),
        (q_hbm.at[0, :, span(enc)], q_buf.at[span(0)]),
        (v_hbm, v_buf),
        (g_hbm.at[0, :, span(enc)], g_buf.at[span(0)]),
    ]
    loads = [pltpu.make_async_copy(a, b, load_sem.at[i]) for i, (a, b) in enumerate(loads)]
    for load in loads:
        load.start()
    for load in loads[:3]:
        load.wait()

    wide_line[...] = jnp.zeros_like(wide_line)
    wide_line[:, 0:table] = line[...]
    bias_map[...] = spread_bias(wide_line[...])
    bias_sum[...] = jnp.zeros_like(bias_sum)

    pl.semaphore_wait(barrier, n_enc - 1 + total - 1)

    def q_copy(step):
        return pltpu.make_async_remote_copy(
            q_hbm.at[0, :, span(to_peer(step))], q_buf.at[span(step)],
            q_send.at[step], q_recv.at[step], (dp, seq, to_peer(step)), MESH,
        )

    def g_copy(step):
        return pltpu.make_async_remote_copy(
            g_hbm.at[0, :, span(to_peer(step))], g_buf.at[span(step)],
            g_send.at[step], g_recv.at[step], (dp, seq, to_peer(step)), MESH,
        )

    def c_copy(step, column):
        return pltpu.make_async_remote_copy(
            c_buf.at[span(step)], context_out.at[0, :, span(column)],
            c_send.at[step], c_recv.at[step], (dp, seq, from_peer(step)), MESH,
        )

    def dq_copy(step, column):
        return pltpu.make_async_remote_copy(
            dq_buf.at[span(step)], query_out.at[0, :, span(column)],
            dq_send.at[step], dq_recv.at[step], (dp, seq, from_peer(step)), MESH,
        )

    def b_copy(step, place):
        return pltpu.make_async_remote_copy(
            bias_row, parts.at[place],
            b_send.at[step], b_recv.at[step], group_at(other(step)), MESH,
        )

    def send_inputs(step):
        q_copy(step).start()
        g_copy(step).start()

    each(1, n_enc, send_inputs)

    for load in loads[3:]:
        load.wait()
    for p in range(pool):
        k_turn[:, p * PASSAGE : (p + 1) * PASSAGE] = k_buf[p * PASSAGE : (p + 1) * PASSAGE, :].T
        v_turn[:, p * PASSAGE : (p + 1) * PASSAGE] = v_buf[p * PASSAGE : (p + 1) * PASSAGE, :].T

    def weigh(step):
        source = from_peer(step)
        s_buf[...] = dot(k_buf[...], q_buf[span(step), :], 1, 1)
        d_buf[...] = dot(v_buf[...], g_buf[span(step), :], 1, 1)
        lane = lax.broadcasted_iota(jnp.int32, (8, ROWS), 1)
        sub = lax.broadcasted_iota(jnp.int32, (8, ROWS), 0)
        first = lane < BLOCK_LEN
        count_a, count_b = counts[source, 0], counts[source, 1]
        count = jnp.where(first, count_a, count_b)
        mask = jnp.full((8, ROWS), NEG_FILL, F32)
        for j in range(slots):
            picked = jnp.where(first, ids[source, 0, j], ids[source, 1, j])
            mask = jnp.where((picked == sub) & (count > j), 0.0, mask)

        def tile(p):
            return pl.ds(p * PASSAGE, PASSAGE)

        def group(x):
            return x.reshape(PASSAGE // 8, 8, ROWS)

        top = jnp.full((8, ROWS), 2 * NEG_FILL, F32)
        for p in range(pool):
            x = s_buf[tile(p), :] * (SCALE * LOG2E) + (bias_map[...] + mask[p : p + 1, :])
            s_buf[tile(p), :] = x
            top = jnp.maximum(top, jnp.max(group(x), axis=0))
        top = jnp.max(top, axis=0, keepdims=True)
        sums = jnp.zeros((8, ROWS), F32)
        dots = jnp.zeros((8, ROWS), F32)
        for p in range(pool):
            e = jnp.exp2(s_buf[tile(p), :] - top)
            s_buf[tile(p), :] = e
            sums = sums + jnp.sum(group(e), axis=0)
            dots = dots + jnp.sum(group(e * d_buf[tile(p), :]), axis=0)
        sums = jnp.sum(sums, axis=0, keepdims=True)
        inverse = jnp.where(count[0:1, :] > 0, 1.0 / sums, 0.0)
        delta = jnp.sum(dots, axis=0, keepdims=True) * inverse
        bias_here = bias_sum[...]
        for p in range(pool):
            w = s_buf[tile(p), :] * inverse
            ds = w * (d_buf[tile(p), :] - delta)
            w_all[tile(p), span(step)] = w.astype(BF16)
            ds_all[tile(p), span(step)] = ds.astype(BF16)
            bias_here = bias_here + ds
        bias_sum[...] = bias_here

    def give_back(step):
        c_turn = dot(v_turn[...], w_all[:, span(step)], 1, 0)
        c_buf[span(step), :] = c_turn.T.astype(BF16)
        dq_turn = dot(k_turn[...], ds_all[:, span(step)], 1, 0) * SCALE
        dq_buf[span(step), :] = dq_turn.T.astype(BF16)

    weigh(0)
    give_back(0)
    own = [
        pltpu.make_async_copy(c_buf.at[span(0)], context_out.at[0, :, span(enc)], own_sem.at[0]),
        pltpu.make_async_copy(dq_buf.at[span(0)], query_out.at[0, :, span(enc)], own_sem.at[1]),
    ]
    for copy in own:
        copy.start()

    def one_source(step):
        q_copy(step).wait_recv()
        g_copy(step).wait_recv()
        weigh(step)
        give_back(step)
        c_copy(step, enc).start()
        dq_copy(step, enc).start()

    each(1, n_enc, one_source)

    bias_row[...] = fold_bias(bias_sum[...])
    each(1, total, lambda step: b_copy(step, flat).start())

    dk_buf[...] = (dot(ds_all[...], q_buf[...], 1, 0) * SCALE).astype(BF16)
    key_store = pltpu.make_async_copy(dk_buf, key_out, store_sem.at[0])
    key_store.start()
    dv_buf[...] = dot(w_all[...], g_buf[...], 1, 0).astype(BF16)
    value_store = pltpu.make_async_copy(dv_buf, value_out, store_sem.at[1])
    value_store.start()

    parts[flat] = bias_row[...]

    def end_bias(step):
        b_copy(step, lax.rem(flat + (total - step), total)).wait_recv()

    each(1, total, end_bias)
    bias_total = parts[0]
    for place in range(1, total):
        bias_total = bias_total + parts[place]
    line[...] = bias_total[:, 0:table]
    bias_store = pltpu.make_async_copy(line, bias_out, store_sem.at[2])
    bias_store.start()

    def end_sends(step):
        q_copy(step).wait_send()
        g_copy(step).wait_send()
        c_copy(step, enc).wait_send()
        dq_copy(step, enc).wait_send()
        c_copy(step, to_peer(step)).wait_recv()
        dq_copy(step, to_peer(step)).wait_recv()

    each(1, n_enc, end_sends)
    each(1, total, lambda step: b_copy(step, flat).wait_send())
    for copy in own:
        copy.wait()
    key_store.wait()
    value_store.wait()
    bias_store.wait()


def local(n_dp, n_seq, n_enc, queries, cotangent, key_pool, value_pool, counts, neighbour_ids, rel_bias):
    pool = key_pool.shape[2]
    tokens = pool * PASSAGE
    slots = neighbour_ids.shape[-1]
    table = rel_bias.shape[1]
    total = n_dp * n_seq
    all_rows = n_enc * ROWS
    anywhere = pl.BlockSpec(memory_space=pl.ANY)
    context, query_grad, key_grad, value_grad, bias_grad = pl.pallas_call(
        functools.partial(kernel, n_dp, n_seq, n_enc, pool, slots),
        out_shape=[
            jax.ShapeDtypeStruct(queries.shape, BF16),
            jax.ShapeDtypeStruct(queries.shape, BF16),
            jax.ShapeDtypeStruct((tokens, HEAD_DIM), BF16),
            jax.ShapeDtypeStruct((tokens, HEAD_DIM), BF16),
            jax.ShapeDtypeStruct(rel_bias.shape, F32),
        ],
        in_specs=[anywhere] * 7,
        out_specs=[anywhere] * 5,
        scratch_shapes=[
            pltpu.VMEM((all_rows, HEAD_DIM), BF16),
            pltpu.VMEM((all_rows, HEAD_DIM), BF16),
            pltpu.VMEM((tokens, HEAD_DIM), BF16),
            pltpu.VMEM((tokens, HEAD_DIM), BF16),
            pltpu.VMEM((HEAD_DIM, tokens), BF16),
            pltpu.VMEM((HEAD_DIM, tokens), BF16),
            pltpu.SMEM(counts.shape, jnp.int32),
            pltpu.SMEM(neighbour_ids.shape, jnp.int32),
            pltpu.VMEM((1, table), F32),
            pltpu.VMEM((1, WIDE), F32),
            pltpu.VMEM((PASSAGE, ROWS), F32),
            pltpu.VMEM((tokens, ROWS), F32),
            pltpu.VMEM((tokens, ROWS), F32),
            pltpu.VMEM((tokens, all_rows), BF16),
            pltpu.VMEM((tokens, all_rows), BF16),
            pltpu.VMEM((PASSAGE, ROWS), F32),
            pltpu.VMEM((all_rows, HEAD_DIM), BF16),
            pltpu.VMEM((all_rows, HEAD_DIM), BF16),
            pltpu.VMEM((tokens, HEAD_DIM), BF16),
            pltpu.VMEM((tokens, HEAD_DIM), BF16),
            pltpu.VMEM((total, 1, WIDE), F32),
            pltpu.VMEM((1, WIDE), F32),
            pltpu.SemaphoreType.DMA((7,)),
            pltpu.SemaphoreType.DMA((2,)),
            pltpu.SemaphoreType.DMA((3,)),
        ]
        + [pltpu.SemaphoreType.DMA((n_enc,))] * 8
        + [pltpu.SemaphoreType.DMA((total,))] * 2,
        compiler_params=pltpu.CompilerParams(
            collective_id=0, has_side_effects=True, vmem_limit_bytes=48 * 1024 * 1024
        ),
        name="retrieval_attention",
    )(
        queries,
        cotangent,
        key_pool.reshape(tokens, HEAD_DIM),
        value_pool.reshape(tokens, HEAD_DIM),
        counts,
        neighbour_ids,
        rel_bias,
    )
    return (
        context,
        query_grad,
        key_grad.reshape(key_pool.shape),
        value_grad.reshape(value_pool.shape),
        bias_grad,
    )


def solution(mesh):
    in_specs = (
        P(("dp", "enc"), "seq", None),
        P(("dp", "enc"), "seq", None),
        P("dp", "seq", None, None, "enc"),
        P("dp", "seq", None, None, "enc"),
        P("dp", "seq"),
        P("dp", "seq", None),
        P("enc", None),
    )
    out_specs = (
        P(("dp", "enc"), "seq", None),
        P(("dp", "enc"), "seq", None),
        P("dp", "seq", None, None, "enc"),
        P("dp", "seq", None, None, "enc"),
        P("enc", None),
    )
    body = functools.partial(local, mesh.shape["dp"], mesh.shape["seq"], mesh.shape["enc"])
    return jax.shard_map(body, mesh=mesh, in_specs=in_specs, out_specs=out_specs, check_vma=False)
```

```python
import functools
import math

import jax
import jax.numpy as jnp
from jax import lax
from jax.experimental import pallas as pl
from jax.experimental.pallas import tpu as pltpu
from jax.sharding import PartitionSpec as P

HEAD_DIM = 128
BLOCK_LEN = 64
PASSAGE = 128
ROWS = 128
WIDE = 256

NEG_FILL = -1e30
SCALE = 1.0 / math.sqrt(HEAD_DIM)
LOG2E = math.log2(math.e)
F32 = jnp.float32
BF16 = jnp.bfloat16
MESH = pl.DeviceIdType.MESH


def each(low, high, body):
    if high - low <= 8:
        for step in range(low, high):
            body(step)
    else:

        def one(step, carry):
            body(step)
            return carry

        lax.fori_loop(low, high, one, 0)


def span(index):
    if isinstance(index, int):
        return pl.ds(index * ROWS, ROWS)
    return pl.ds(pl.multiple_of(index * ROWS, ROWS), ROWS)


def dot(left, right, left_dim, right_dim):
    return lax.dot_general(
        left, right, (((left_dim,), (right_dim,)), ((), ())), preferred_element_type=F32
    )


def spread_bias(line):
    rows = jnp.broadcast_to(line * LOG2E, (8, WIDE))
    sub = lax.broadcasted_iota(jnp.int32, (8, WIDE), 0)
    rows = pltpu.roll(rows, WIDE - (BLOCK_LEN - 1), 1)
    for bit in (1, 2, 4):
        rows = jnp.where((sub & bit) != 0, pltpu.roll(rows, bit, 1), rows)
    groups = [rows] + [pltpu.roll(rows, 8 * k, 1) for k in range(1, BLOCK_LEN // 8)]
    block = jnp.concatenate([group[:, :PASSAGE] for group in groups], axis=0)
    return jnp.concatenate([block, block], axis=0).T


def fold_bias(total):
    turned = total.T
    block = turned[:BLOCK_LEN] + turned[BLOCK_LEN:]
    block = jnp.concatenate([block, jnp.zeros((BLOCK_LEN, WIDE - PASSAGE), F32)], axis=1)
    for half in (32, 16, 8):
        block = pltpu.roll(block[:half], half, 1) + block[half : 2 * half]
    sub = lax.broadcasted_iota(jnp.int32, (8, WIDE), 0)
    for bit in (4, 2, 1):
        block = jnp.where((sub & bit) == 0, pltpu.roll(block, bit, 1), block)
    return jnp.sum(block, axis=0, keepdims=True)


def kernel(
    n_dp, n_seq, n_enc, pool, slots,
    q_hbm, g_hbm, k_hbm, v_hbm, count_hbm, id_hbm, bias_hbm,
    context_out, query_out, key_out, value_out, bias_out,
    q_buf, g_buf, k_buf, v_buf, k_turn, v_turn, counts, ids, line, wide_line, bias_map,
    s_buf, d_buf, w_all, ds_all, bias_sum, c_buf, dq_buf, dk_buf, dv_buf, parts, bias_row,
    load_sem, own_sem, store_sem,
    q_send, q_recv, g_send, g_recv, c_send, c_recv, dq_send, dq_recv, b_send, b_recv,
):
    dp, seq, enc = lax.axis_index("dp"), lax.axis_index("seq"), lax.axis_index("enc")
    total = n_dp * n_seq
    flat = dp * n_seq + seq
    table = line.shape[1]

    paired = n_enc <= 8 and n_enc & (n_enc - 1) == 0

    def partner(step):
        place = enc
        bit = 1
        while bit < n_enc:
            if step & bit:
                place = place + bit * (1 - 2 * lax.rem(enc // bit, 2))
            bit *= 2
        return place

    def to_peer(step):
        return partner(step) if paired else lax.rem(enc + step, n_enc)

    def from_peer(step):
        return partner(step) if paired else lax.rem(enc + (n_enc - step), n_enc)

    def group_at(place):
        return (place // n_seq, lax.rem(place, n_seq), enc)

    def other(step):
        return lax.rem(flat + step, total)

    barrier = pltpu.get_barrier_semaphore()

    def greet(step):
        pl.semaphore_signal(barrier, inc=1, device_id=(dp, seq, to_peer(step)), device_id_type=MESH)

    def greet_group(step):
        pl.semaphore_signal(barrier, inc=1, device_id=group_at(other(step)), device_id_type=MESH)

    each(1, n_enc, greet)
    each(1, total, greet_group)

    loads = [
        (bias_hbm, line),
        (count_hbm, counts),
        (id_hbm, ids),
        (k_hbm, k_buf),
        (q_hbm.at[0, :, span(enc)], q_buf.at[span(0)]),
        (v_hbm, v_buf),
        (g_hbm.at[0, :, span(enc)], g_buf.at[span(0)]),
    ]
    loads = [pltpu.make_async_copy(a, b, load_sem.at[i]) for i, (a, b) in enumerate(loads)]
    for load in loads:
        load.start()
    pl.semaphore_wait(barrier, n_enc - 1 + total - 1)

    def q_copy(step):
        return pltpu.make_async_remote_copy(
            q_hbm.at[0, :, span(to_peer(step))], q_buf.at[span(step)],
            q_send.at[step], q_recv.at[step], (dp, seq, to_peer(step)), MESH,
        )

    def g_copy(step):
        return pltpu.make_async_remote_copy(
            g_hbm.at[0, :, span(to_peer(step))], g_buf.at[span(step)],
            g_send.at[step], g_recv.at[step], (dp, seq, to_peer(step)), MESH,
        )

    def c_copy(step, column):
        return pltpu.make_async_remote_copy(
            c_buf.at[span(step)], context_out.at[0, :, span(column)],
            c_send.at[step], c_recv.at[step], (dp, seq, from_peer(step)), MESH,
        )

    def dq_copy(step, column):
        return pltpu.make_async_remote_copy(
            dq_buf.at[span(step)], query_out.at[0, :, span(column)],
            dq_send.at[step], dq_recv.at[step], (dp, seq, from_peer(step)), MESH,
        )

    def b_copy(step, place):
        return pltpu.make_async_remote_copy(
            bias_row, parts.at[place],
            b_send.at[step], b_recv.at[step], group_at(other(step)), MESH,
        )

    def send_inputs(step):
        q_copy(step).start()
        g_copy(step).start()

    each(1, n_enc, lambda step: send_inputs(n_enc - step))

    for load in loads:
        load.wait()
    wide_line[...] = jnp.zeros_like(wide_line)
    wide_line[:, 0:table] = line[...]
    bias_map[...] = spread_bias(wide_line[...])
    bias_sum[...] = jnp.zeros_like(bias_sum)
    for p in range(pool):
        k_turn[:, p * PASSAGE : (p + 1) * PASSAGE] = k_buf[p * PASSAGE : (p + 1) * PASSAGE, :].T
        v_turn[:, p * PASSAGE : (p + 1) * PASSAGE] = v_buf[p * PASSAGE : (p + 1) * PASSAGE, :].T

    def weigh(step):
        source = from_peer(step)
        query, grad = q_buf[span(step), :], g_buf[span(step), :]
        lane = lax.broadcasted_iota(jnp.int32, (8, ROWS), 1)
        sub = lax.broadcasted_iota(jnp.int32, (8, ROWS), 0)
        first = lane < BLOCK_LEN
        count_a, count_b = counts[0, source], counts[1, source]
        count = jnp.where(first, count_a, count_b)
        mask = jnp.full((8, ROWS), NEG_FILL, F32)
        for j in range(slots):
            picked = jnp.where(first, ids[source, 0, j], ids[source, 1, j])
            mask = jnp.where((picked == sub) & (count > j), 0.0, mask)

        live = count[0:1, :] > 0

        def tile(p):
            return pl.ds(p * PASSAGE, PASSAGE)

        def group(x):
            return x.reshape(PASSAGE // 8, 8, ROWS)

        top = jnp.full((1, ROWS), 2 * NEG_FILL, F32)
        for pair in range(0, pool, 2):
            raw = dot(k_buf[pl.ds(pair * PASSAGE, 2 * PASSAGE), :], query, 1, 1)
            for p in (pair, pair + 1):
                x = raw[(p - pair) * PASSAGE : (p - pair + 1) * PASSAGE]
                x = x * (SCALE * LOG2E) + bias_map[...]
                s_buf[tile(p), :] = x
                highest = jnp.max(jnp.max(group(x), axis=0), axis=0, keepdims=True)
                top = jnp.maximum(top, highest + mask[p : p + 1, :])
        shift = mask - jnp.where(live, top, 0.0)
        sums = jnp.zeros((8, ROWS), F32)
        dots = jnp.zeros((8, ROWS), F32)
        for pair in range(0, pool, 2):
            raw = dot(v_buf[pl.ds(pair * PASSAGE, 2 * PASSAGE), :], grad, 1, 1)
            for p in (pair, pair + 1):
                d = raw[(p - pair) * PASSAGE : (p - pair + 1) * PASSAGE]
                e = jnp.exp2(s_buf[tile(p), :] + shift[p : p + 1, :])
                s_buf[tile(p), :] = e
                d_buf[tile(p), :] = d
                sums = sums + jnp.sum(group(e), axis=0)
                dots = dots + jnp.sum(group(e * d), axis=0)
        sums = jnp.sum(sums, axis=0, keepdims=True)
        inverse = jnp.where(live, 1.0 / sums, 0.0)
        delta = jnp.sum(dots, axis=0, keepdims=True) * inverse
        bias_here = bias_sum[...]
        for p in range(pool):
            w = s_buf[tile(p), :] * inverse
            ds = w * (d_buf[tile(p), :] - delta)
            w_all[tile(p), span(step)] = w.astype(BF16)
            ds_all[tile(p), span(step)] = ds.astype(BF16)
            bias_here = bias_here + ds
        bias_sum[...] = bias_here

    def give_back(step):
        c_turn = dot(v_turn[...], w_all[:, span(step)], 1, 0)
        c_buf[span(step), :] = c_turn.T.astype(BF16)
        dq_turn = dot(k_turn[...], ds_all[:, span(step)], 1, 0) * SCALE
        dq_buf[span(step), :] = dq_turn.T.astype(BF16)

    weigh(0)
    give_back(0)
    own = [
        pltpu.make_async_copy(c_buf.at[span(0)], context_out.at[0, :, span(enc)], own_sem.at[0]),
        pltpu.make_async_copy(dq_buf.at[span(0)], query_out.at[0, :, span(enc)], own_sem.at[1]),
    ]
    for copy in own:
        copy.start()

    def arrive(step):
        q_copy(step).wait_recv()
        g_copy(step).wait_recv()

    def reply(step):
        give_back(step)
        c_copy(step, enc).start()
        dq_copy(step, enc).start()

    def one_source(step):
        weigh(step)
        reply(step)

    each(1, n_enc, arrive)
    each(2, n_enc, lambda step: one_source(n_enc + 1 - step))
    weigh(1)
    bias_row[...] = fold_bias(bias_sum[...])
    each(1, total, lambda step: b_copy(step, flat).start())
    reply(1)

    dk_buf[...] = (dot(ds_all[...], q_buf[...], 1, 0) * SCALE).astype(BF16)
    key_store = pltpu.make_async_copy(dk_buf, key_out, store_sem.at[0])
    key_store.start()
    dv_buf[...] = dot(w_all[...], g_buf[...], 1, 0).astype(BF16)
    value_store = pltpu.make_async_copy(dv_buf, value_out, store_sem.at[1])
    value_store.start()

    parts[flat] = bias_row[...]

    def end_bias(step):
        b_copy(step, lax.rem(flat + (total - step), total)).wait_recv()

    each(1, total, end_bias)
    bias_total = parts[0]
    for place in range(1, total):
        bias_total = bias_total + parts[place]
    line[...] = bias_total[:, 0:table]
    bias_store = pltpu.make_async_copy(line, bias_out, store_sem.at[2])
    bias_store.start()

    def end_sends(step):
        q_copy(step).wait_send()
        g_copy(step).wait_send()
        c_copy(step, enc).wait_send()
        dq_copy(step, enc).wait_send()
        c_copy(step, to_peer(step)).wait_recv()
        dq_copy(step, to_peer(step)).wait_recv()

    each(1, n_enc, end_sends)
    each(1, total, lambda step: b_copy(step, flat).wait_send())
    for copy in own:
        copy.wait()
    key_store.wait()
    value_store.wait()
    bias_store.wait()


def write_out(*refs):
    sources, targets, sem = refs[:5], refs[5:10], refs[10]
    copies = [
        pltpu.make_async_copy(source, target, sem.at[i])
        for i, (source, target) in enumerate(zip(sources, targets))
    ]
    for copy in copies:
        copy.start()
    for copy in copies:
        copy.wait()


def local(n_dp, n_seq, n_enc, queries, cotangent, key_pool, value_pool, counts, neighbour_ids, rel_bias):
    pool = key_pool.shape[2]
    tokens = pool * PASSAGE
    slots = neighbour_ids.shape[-1]
    table = rel_bias.shape[1]
    total = n_dp * n_seq
    all_rows = n_enc * ROWS
    anywhere = pl.BlockSpec(memory_space=pl.ANY)
    held = pl.BlockSpec(memory_space=pltpu.HBM)
    results = pl.pallas_call(
        functools.partial(kernel, n_dp, n_seq, n_enc, pool, slots),
        out_shape=[
            jax.ShapeDtypeStruct(queries.shape, BF16),
            jax.ShapeDtypeStruct(queries.shape, BF16),
            jax.ShapeDtypeStruct((tokens, HEAD_DIM), BF16),
            jax.ShapeDtypeStruct((tokens, HEAD_DIM), BF16),
            jax.ShapeDtypeStruct(rel_bias.shape, F32),
        ],
        in_specs=[held] * 7,
        out_specs=[anywhere] * 5,
        scratch_shapes=[
            pltpu.VMEM((all_rows, HEAD_DIM), BF16),
            pltpu.VMEM((all_rows, HEAD_DIM), BF16),
            pltpu.VMEM((tokens, HEAD_DIM), BF16),
            pltpu.VMEM((tokens, HEAD_DIM), BF16),
            pltpu.VMEM((HEAD_DIM, tokens), BF16),
            pltpu.VMEM((HEAD_DIM, tokens), BF16),
            pltpu.SMEM(counts.shape[::-1], jnp.int32),
            pltpu.SMEM(neighbour_ids.shape, jnp.int32),
            pltpu.VMEM((1, table), F32),
            pltpu.VMEM((1, WIDE), F32),
            pltpu.VMEM((PASSAGE, ROWS), F32),
            pltpu.VMEM((tokens, ROWS), F32),
            pltpu.VMEM((tokens, ROWS), F32),
            pltpu.VMEM((tokens, all_rows), BF16),
            pltpu.VMEM((tokens, all_rows), BF16),
            pltpu.VMEM((PASSAGE, ROWS), F32),
            pltpu.VMEM((all_rows, HEAD_DIM), BF16),
            pltpu.VMEM((all_rows, HEAD_DIM), BF16),
            pltpu.VMEM((tokens, HEAD_DIM), BF16),
            pltpu.VMEM((tokens, HEAD_DIM), BF16),
            pltpu.VMEM((total, 1, WIDE), F32),
            pltpu.VMEM((1, WIDE), F32),
            pltpu.SemaphoreType.DMA((7,)),
            pltpu.SemaphoreType.DMA((2,)),
            pltpu.SemaphoreType.DMA((3,)),
        ]
        + [pltpu.SemaphoreType.DMA((n_enc,))] * 8
        + [pltpu.SemaphoreType.DMA((total,))] * 2,
        compiler_params=pltpu.CompilerParams(
            collective_id=0, has_side_effects=True, vmem_limit_bytes=48 * 1024 * 1024
        ),
        name="retrieval_attention",
    )(
        pltpu.with_memory_space_constraint(queries, pltpu.HBM),
        pltpu.with_memory_space_constraint(cotangent, pltpu.HBM),
        pltpu.with_memory_space_constraint(key_pool.reshape(tokens, HEAD_DIM), pltpu.HBM),
        pltpu.with_memory_space_constraint(value_pool.reshape(tokens, HEAD_DIM), pltpu.HBM),
        pltpu.with_memory_space_constraint(counts.T, pltpu.HBM),
        pltpu.with_memory_space_constraint(neighbour_ids, pltpu.HBM),
        pltpu.with_memory_space_constraint(rel_bias, pltpu.HBM),
    )
    context, query_grad, key_grad, value_grad, bias_grad = pl.pallas_call(
        write_out,
        out_shape=[jax.ShapeDtypeStruct(x.shape, x.dtype) for x in results],
        in_specs=[anywhere] * 5,
        out_specs=[held] * 5,
        scratch_shapes=[pltpu.SemaphoreType.DMA((5,))],
        name="write_out",
    )(*results)
    return (
        context,
        query_grad,
        key_grad.reshape(key_pool.shape),
        value_grad.reshape(value_pool.shape),
        bias_grad,
    )


def solution(mesh):
    in_specs = (
        P(("dp", "enc"), "seq", None),
        P(("dp", "enc"), "seq", None),
        P("dp", "seq", None, None, "enc"),
        P("dp", "seq", None, None, "enc"),
        P("dp", "seq"),
        P("dp", "seq", None),
        P("enc", None),
    )
    out_specs = (
        P(("dp", "enc"), "seq", None),
        P(("dp", "enc"), "seq", None),
        P("dp", "seq", None, None, "enc"),
        P("dp", "seq", None, None, "enc"),
        P("enc", None),
    )
    body = functools.partial(local, mesh.shape["dp"], mesh.shape["seq"], mesh.shape["enc"])
    return jax.shard_map(body, mesh=mesh, in_specs=in_specs, out_specs=out_specs, check_vma=False)
```

```python
import functools
import math

import jax
import jax.numpy as jnp
from jax import lax
from jax.experimental import pallas as pl
from jax.experimental.pallas import tpu as pltpu
from jax.sharding import PartitionSpec as P

HEAD_DIM = 128
BLOCK_LEN = 64
PASSAGE = 128
ROWS = 128
WIDE = 256

NEG_FILL = -1e30
SCALE = 1.0 / math.sqrt(HEAD_DIM)
LOG2E = math.log2(math.e)
F32 = jnp.float32
BF16 = jnp.bfloat16
MESH = pl.DeviceIdType.MESH


def each(low, high, body, unrolled=8):
    if high - low <= unrolled:
        for step in range(low, high):
            body(step)
    else:

        def one(step, carry):
            body(step)
            return carry

        lax.fori_loop(low, high, one, 0)


def span(index, width=1):
    if isinstance(index, int):
        return pl.ds(index * ROWS, width * ROWS)
    return pl.ds(pl.multiple_of(index * ROWS, ROWS), width * ROWS)


def dot(left, right, left_dim, right_dim):
    return lax.dot_general(
        left, right, (((left_dim,), (right_dim,)), ((), ())), preferred_element_type=F32
    )


def spread_bias(line):
    rows = jnp.broadcast_to(line * LOG2E, (8, WIDE))
    sub = lax.broadcasted_iota(jnp.int32, (8, WIDE), 0)
    rows = pltpu.roll(rows, WIDE - (BLOCK_LEN - 1), 1)
    for bit in (1, 2, 4):
        rows = jnp.where((sub & bit) != 0, pltpu.roll(rows, bit, 1), rows)
    groups = [rows] + [pltpu.roll(rows, 8 * k, 1) for k in range(1, BLOCK_LEN // 8)]
    block = jnp.concatenate([group[:, :PASSAGE] for group in groups], axis=0)
    return jnp.concatenate([block, block], axis=0).T


def fold_bias(total):
    parts = [total[:, at : at + ROWS] for at in range(0, total.shape[1], ROWS)]
    turned = functools.reduce(jnp.add, parts).T
    block = turned[:BLOCK_LEN] + turned[BLOCK_LEN:]
    block = jnp.concatenate([block, jnp.zeros((BLOCK_LEN, WIDE - PASSAGE), F32)], axis=1)
    for half in (32, 16, 8):
        block = pltpu.roll(block[:half], half, 1) + block[half : 2 * half]
    sub = lax.broadcasted_iota(jnp.int32, (8, WIDE), 0)
    for bit in (4, 2, 1):
        block = jnp.where((sub & bit) == 0, pltpu.roll(block, bit, 1), block)
    return jnp.sum(block, axis=0, keepdims=True)


def kernel(
    n_dp, n_seq, n_enc, pool, slots,
    q_hbm, g_hbm, k_hbm, v_hbm, count_hbm, id_hbm, bias_hbm,
    context_out, query_out, key_out, value_out, bias_out,
    q_buf, g_buf, k_buf, v_buf, k_turn, v_turn, counts, ids, line, wide_line, bias_map,
    s_buf, d_buf, w_all, ds_all, bias_sum, c_buf, dq_buf, dk_buf, dv_buf, parts, bias_row,
    load_sem, own_sem, store_sem,
    q_send, q_recv, g_send, g_recv, c_send, c_recv, dq_send, dq_recv, b_send, b_recv,
):
    dp, seq, enc = lax.axis_index("dp"), lax.axis_index("seq"), lax.axis_index("enc")
    total = n_dp * n_seq
    flat = dp * n_seq + seq
    table = line.shape[1]

    together = 2 if n_enc % 2 == 0 else 1
    groups = n_enc // together
    paired = n_enc <= 8 and n_enc & (n_enc - 1) == 0

    def partner(step):
        place = enc
        bit = 1
        while bit < n_enc:
            if step & bit:
                place = place + bit * (1 - 2 * lax.rem(enc // bit, 2))
            bit *= 2
        return place

    def to_peer(step):
        return partner(step) if paired else lax.rem(enc + step, n_enc)

    def from_peer(step):
        return partner(step) if paired else lax.rem(enc + (n_enc - step), n_enc)

    def group_at(place):
        return (place // n_seq, lax.rem(place, n_seq), enc)

    def other(step):
        return lax.rem(flat + step, total)

    barrier = pltpu.get_barrier_semaphore()

    def greet(step):
        pl.semaphore_signal(barrier, inc=1, device_id=(dp, seq, to_peer(step)), device_id_type=MESH)

    def greet_group(step):
        pl.semaphore_signal(barrier, inc=1, device_id=group_at(other(step)), device_id_type=MESH)

    each(1, n_enc, greet)
    each(1, total, greet_group)

    loads = [
        (bias_hbm, line),
        (count_hbm, counts),
        (id_hbm, ids),
        (k_hbm, k_buf),
        (q_hbm.at[0, :, span(enc)], q_buf.at[span(0)]),
        (v_hbm, v_buf),
        (g_hbm.at[0, :, span(enc)], g_buf.at[span(0)]),
    ]
    loads = [pltpu.make_async_copy(a, b, load_sem.at[i]) for i, (a, b) in enumerate(loads)]
    for load in loads:
        load.start()
    pl.semaphore_wait(barrier, n_enc - 1 + total - 1)

    def q_copy(step):
        return pltpu.make_async_remote_copy(
            q_hbm.at[0, :, span(to_peer(step))], q_buf.at[span(step)],
            q_send.at[step], q_recv.at[step], (dp, seq, to_peer(step)), MESH,
        )

    def g_copy(step):
        return pltpu.make_async_remote_copy(
            g_hbm.at[0, :, span(to_peer(step))], g_buf.at[span(step)],
            g_send.at[step], g_recv.at[step], (dp, seq, to_peer(step)), MESH,
        )

    def c_copy(step, column):
        return pltpu.make_async_remote_copy(
            c_buf.at[span(step)], context_out.at[0, :, span(column)],
            c_send.at[step], c_recv.at[step], (dp, seq, from_peer(step)), MESH,
        )

    def dq_copy(step, column):
        return pltpu.make_async_remote_copy(
            dq_buf.at[span(step)], query_out.at[0, :, span(column)],
            dq_send.at[step], dq_recv.at[step], (dp, seq, from_peer(step)), MESH,
        )

    def b_copy(step, place):
        return pltpu.make_async_remote_copy(
            bias_row, parts.at[place],
            b_send.at[step], b_recv.at[step], group_at(other(step)), MESH,
        )

    def send_inputs(step):
        q_copy(step).start()
        g_copy(step).start()

    each(1, n_enc, lambda step: send_inputs(n_enc - step))

    for load in loads:
        load.wait()
    wide_line[...] = jnp.zeros_like(wide_line)
    wide_line[:, 0:table] = line[...]
    bias_one = spread_bias(wide_line[...])
    for at in range(together):
        bias_map[:, span(at)] = bias_one
    bias_sum[...] = jnp.zeros_like(bias_sum)
    for p in range(pool):
        k_turn[:, p * PASSAGE : (p + 1) * PASSAGE] = k_buf[p * PASSAGE : (p + 1) * PASSAGE, :].T
        v_turn[:, p * PASSAGE : (p + 1) * PASSAGE] = v_buf[p * PASSAGE : (p + 1) * PASSAGE, :].T

    def allowed(step):
        source = from_peer(step)
        lane = lax.broadcasted_iota(jnp.int32, (8, ROWS), 1)
        sub = lax.broadcasted_iota(jnp.int32, (8, ROWS), 0)
        first = lane < BLOCK_LEN
        count = jnp.where(first, counts[0, source], counts[1, source])
        mask = jnp.full((8, ROWS), NEG_FILL, F32)
        for j in range(slots):
            picked = jnp.where(first, ids[source, 0, j], ids[source, 1, j])
            mask = jnp.where((picked == sub) & (count > j), 0.0, mask)
        return mask, count

    def weigh(batch):
        at = batch * together
        here = span(at, together)
        columns = together * ROWS
        query, grad = q_buf[here, :], g_buf[here, :]
        masks = [allowed(at + k) for k in range(together)]
        mask = jnp.concatenate([pair[0] for pair in masks], axis=1)
        count = jnp.concatenate([pair[1] for pair in masks], axis=1)
        live = count[0:1, :] > 0

        def tile(p):
            return pl.ds(p * PASSAGE, PASSAGE)

        def group(x):
            return x.reshape(PASSAGE // 8, 8, columns)

        top = jnp.full((1, columns), 2 * NEG_FILL, F32)
        for pair in range(0, pool, 2):
            raw = dot(k_buf[pl.ds(pair * PASSAGE, 2 * PASSAGE), :], query, 1, 1)
            for p in (pair, pair + 1):
                x = raw[(p - pair) * PASSAGE : (p - pair + 1) * PASSAGE]
                x = x * (SCALE * LOG2E) + bias_map[...]
                s_buf[tile(p), :] = x
                highest = jnp.max(jnp.max(group(x), axis=0), axis=0, keepdims=True)
                top = jnp.maximum(top, highest + mask[p : p + 1, :])
        shift = mask - jnp.where(live, top, 0.0)
        sums = jnp.zeros((8, columns), F32)
        dots = jnp.zeros((8, columns), F32)
        for pair in range(0, pool, 2):
            raw = dot(v_buf[pl.ds(pair * PASSAGE, 2 * PASSAGE), :], grad, 1, 1)
            for p in (pair, pair + 1):
                d = raw[(p - pair) * PASSAGE : (p - pair + 1) * PASSAGE]
                e = jnp.exp2(s_buf[tile(p), :] + shift[p : p + 1, :])
                s_buf[tile(p), :] = e
                d_buf[tile(p), :] = d
                sums = sums + jnp.sum(group(e), axis=0)
                dots = dots + jnp.sum(group(e * d), axis=0)
        sums = jnp.sum(sums, axis=0, keepdims=True)
        inverse = jnp.where(live, 1.0 / sums, 0.0)
        delta = jnp.sum(dots, axis=0, keepdims=True) * inverse
        bias_here = bias_sum[...]
        for p in range(pool):
            w = s_buf[tile(p), :] * inverse
            ds = w * (d_buf[tile(p), :] - delta)
            w_all[tile(p), here] = w.astype(BF16)
            ds_all[tile(p), here] = ds.astype(BF16)
            bias_here = bias_here + ds
        bias_sum[...] = bias_here

    def give_back(batch):
        here = span(batch * together, together)
        c_turn = dot(v_turn[...], w_all[:, here], 1, 0)
        c_buf[here, :] = c_turn.T.astype(BF16)
        each_of(batch, lambda step: c_copy(step, enc).start())
        dq_turn = dot(k_turn[...], ds_all[:, here], 1, 0) * SCALE
        dq_buf[here, :] = dq_turn.T.astype(BF16)
        each_of(batch, lambda step: dq_copy(step, enc).start())

    def each_of(batch, body):
        for k in range(together):
            if not (isinstance(batch, int) and batch * together + k == 0):
                body(batch * together + k)

    def arrive(step):
        q_copy(step).wait_recv()
        g_copy(step).wait_recv()

    def one_batch(batch):
        each_of(batch, arrive)
        weigh(batch)
        give_back(batch)

    one_batch(0)
    own = [
        pltpu.make_async_copy(c_buf.at[span(0)], context_out.at[0, :, span(enc)], own_sem.at[0]),
        pltpu.make_async_copy(dq_buf.at[span(0)], query_out.at[0, :, span(enc)], own_sem.at[1]),
    ]
    for copy in own:
        copy.start()

    def send_bias():
        bias_row[...] = fold_bias(bias_sum[...])
        each(1, total, lambda step: b_copy(step, flat).start())

    last = groups - 1
    each(1, last, one_batch, unrolled=2)
    if last > 0:
        each_of(last, arrive)
        weigh(last)
    send_bias()
    if last > 0:
        give_back(last)

    dk_buf[...] = (dot(ds_all[...], q_buf[...], 1, 0) * SCALE).astype(BF16)
    key_store = pltpu.make_async_copy(dk_buf, key_out, store_sem.at[0])
    key_store.start()
    dv_buf[...] = dot(w_all[...], g_buf[...], 1, 0).astype(BF16)
    value_store = pltpu.make_async_copy(dv_buf, value_out, store_sem.at[1])
    value_store.start()

    parts[flat] = bias_row[...]

    def end_bias(step):
        b_copy(step, lax.rem(flat + (total - step), total)).wait_recv()

    each(1, total, end_bias)
    bias_total = parts[0]
    for place in range(1, total):
        bias_total = bias_total + parts[place]
    line[...] = bias_total[:, 0:table]
    bias_store = pltpu.make_async_copy(line, bias_out, store_sem.at[2])
    bias_store.start()

    def end_sends(step):
        q_copy(step).wait_send()
        g_copy(step).wait_send()
        c_copy(step, enc).wait_send()
        dq_copy(step, enc).wait_send()
        c_copy(step, to_peer(step)).wait_recv()
        dq_copy(step, to_peer(step)).wait_recv()

    each(1, n_enc, end_sends)
    each(1, total, lambda step: b_copy(step, flat).wait_send())
    for copy in own:
        copy.wait()
    key_store.wait()
    value_store.wait()
    bias_store.wait()


def write_out(*refs):
    sources, targets, sem = refs[:5], refs[5:10], refs[10]
    copies = [
        pltpu.make_async_copy(source, target, sem.at[i])
        for i, (source, target) in enumerate(zip(sources, targets))
    ]
    for copy in copies:
        copy.start()
    for copy in copies:
        copy.wait()


def local(n_dp, n_seq, n_enc, queries, cotangent, key_pool, value_pool, counts, neighbour_ids, rel_bias):
    pool = key_pool.shape[2]
    tokens = pool * PASSAGE
    slots = neighbour_ids.shape[-1]
    table = rel_bias.shape[1]
    total = n_dp * n_seq
    all_rows = n_enc * ROWS
    batch_rows = ROWS * (2 if n_enc % 2 == 0 else 1)
    anywhere = pl.BlockSpec(memory_space=pl.ANY)
    held = pl.BlockSpec(memory_space=pltpu.HBM)
    results = pl.pallas_call(
        functools.partial(kernel, n_dp, n_seq, n_enc, pool, slots),
        out_shape=[
            jax.ShapeDtypeStruct(queries.shape, BF16),
            jax.ShapeDtypeStruct(queries.shape, BF16),
            jax.ShapeDtypeStruct((tokens, HEAD_DIM), BF16),
            jax.ShapeDtypeStruct((tokens, HEAD_DIM), BF16),
            jax.ShapeDtypeStruct(rel_bias.shape, F32),
        ],
        in_specs=[held] * 7,
        out_specs=[anywhere] * 5,
        scratch_shapes=[
            pltpu.VMEM((all_rows, HEAD_DIM), BF16),
            pltpu.VMEM((all_rows, HEAD_DIM), BF16),
            pltpu.VMEM((tokens, HEAD_DIM), BF16),
            pltpu.VMEM((tokens, HEAD_DIM), BF16),
            pltpu.VMEM((HEAD_DIM, tokens), BF16),
            pltpu.VMEM((HEAD_DIM, tokens), BF16),
            pltpu.SMEM(counts.shape[::-1], jnp.int32),
            pltpu.SMEM(neighbour_ids.shape, jnp.int32),
            pltpu.VMEM((1, table), F32),
            pltpu.VMEM((1, WIDE), F32),
            pltpu.VMEM((PASSAGE, batch_rows), F32),
            pltpu.VMEM((tokens, batch_rows), F32),
            pltpu.VMEM((tokens, batch_rows), F32),
            pltpu.VMEM((tokens, all_rows), BF16),
            pltpu.VMEM((tokens, all_rows), BF16),
            pltpu.VMEM((PASSAGE, batch_rows), F32),
            pltpu.VMEM((all_rows, HEAD_DIM), BF16),
            pltpu.VMEM((all_rows, HEAD_DIM), BF16),
            pltpu.VMEM((tokens, HEAD_DIM), BF16),
            pltpu.VMEM((tokens, HEAD_DIM), BF16),
            pltpu.VMEM((total, 1, WIDE), F32),
            pltpu.VMEM((1, WIDE), F32),
            pltpu.SemaphoreType.DMA((7,)),
            pltpu.SemaphoreType.DMA((2,)),
            pltpu.SemaphoreType.DMA((3,)),
        ]
        + [pltpu.SemaphoreType.DMA((n_enc,))] * 8
        + [pltpu.SemaphoreType.DMA((total,))] * 2,
        compiler_params=pltpu.CompilerParams(
            collective_id=0, has_side_effects=True, vmem_limit_bytes=48 * 1024 * 1024
        ),
        name="retrieval_attention",
    )(
        pltpu.with_memory_space_constraint(queries, pltpu.HBM),
        pltpu.with_memory_space_constraint(cotangent, pltpu.HBM),
        pltpu.with_memory_space_constraint(key_pool.reshape(tokens, HEAD_DIM), pltpu.HBM),
        pltpu.with_memory_space_constraint(value_pool.reshape(tokens, HEAD_DIM), pltpu.HBM),
        pltpu.with_memory_space_constraint(counts.T, pltpu.HBM),
        pltpu.with_memory_space_constraint(neighbour_ids, pltpu.HBM),
        pltpu.with_memory_space_constraint(rel_bias, pltpu.HBM),
    )
    context, query_grad, key_grad, value_grad, bias_grad = pl.pallas_call(
        write_out,
        out_shape=[jax.ShapeDtypeStruct(x.shape, x.dtype) for x in results],
        in_specs=[anywhere] * 5,
        out_specs=[held] * 5,
        scratch_shapes=[pltpu.SemaphoreType.DMA((5,))],
        compiler_params=pltpu.CompilerParams(vmem_limit_bytes=2 * 1024 * 1024),
        name="write_out",
    )(*results)
    return (
        context,
        query_grad,
        key_grad.reshape(key_pool.shape),
        value_grad.reshape(value_pool.shape),
        bias_grad,
    )


def solution(mesh):
    in_specs = (
        P(("dp", "enc"), "seq", None),
        P(("dp", "enc"), "seq", None),
        P("dp", "seq", None, None, "enc"),
        P("dp", "seq", None, None, "enc"),
        P("dp", "seq"),
        P("dp", "seq", None),
        P("enc", None),
    )
    out_specs = (
        P(("dp", "enc"), "seq", None),
        P(("dp", "enc"), "seq", None),
        P("dp", "seq", None, None, "enc"),
        P("dp", "seq", None, None, "enc"),
        P("enc", None),
    )
    body = functools.partial(local, mesh.shape["dp"], mesh.shape["seq"], mesh.shape["enc"])
    return jax.shard_map(body, mesh=mesh, in_specs=in_specs, out_specs=out_specs, check_vma=False)
```

```python
import functools
import math

import jax
import jax.numpy as jnp
from jax import lax
from jax.experimental import pallas as pl
from jax.experimental.pallas import tpu as pltpu
from jax.sharding import PartitionSpec as P

HEAD_DIM = 128
BLOCK_LEN = 64
PASSAGE = 128
ROWS = 128
WIDE = 256

NEG_FILL = -1e30
SCALE = 1.0 / math.sqrt(HEAD_DIM)
F32 = jnp.float32
BF16 = jnp.bfloat16
MESH = pl.DeviceIdType.MESH


def each(low, high, body, unrolled=8):
    if high - low <= unrolled:
        for step in range(low, high):
            body(step)
    else:

        def one(step, carry):
            body(step)
            return carry

        lax.fori_loop(low, high, one, 0)


def span(index, width=1):
    if isinstance(index, int):
        return pl.ds(index * ROWS, width * ROWS)
    return pl.ds(pl.multiple_of(index * ROWS, ROWS), width * ROWS)


def dot(left, right, left_dim, right_dim):
    return lax.dot_general(
        left, right, (((left_dim,), (right_dim,)), ((), ())), preferred_element_type=F32
    )


def spread_bias(line):
    rows = jnp.broadcast_to(line, (8, WIDE))
    sub = lax.broadcasted_iota(jnp.int32, (8, WIDE), 0)
    rows = pltpu.roll(rows, WIDE - (BLOCK_LEN - 1), 1)
    for bit in (1, 2, 4):
        rows = jnp.where((sub & bit) != 0, pltpu.roll(rows, bit, 1), rows)
    groups = [rows] + [pltpu.roll(rows, 8 * k, 1) for k in range(1, BLOCK_LEN // 8)]
    block = jnp.concatenate([group[:, :PASSAGE] for group in groups], axis=0)
    return jnp.concatenate([block, block], axis=0).T


def fold_bias(total):
    parts = [total[:, at : at + ROWS] for at in range(0, total.shape[1], ROWS)]
    turned = functools.reduce(jnp.add, parts).T
    block = turned[:BLOCK_LEN] + turned[BLOCK_LEN:]
    block = jnp.concatenate([block, jnp.zeros((BLOCK_LEN, WIDE - PASSAGE), F32)], axis=1)
    for half in (32, 16, 8):
        block = pltpu.roll(block[:half], half, 1) + block[half : 2 * half]
    sub = lax.broadcasted_iota(jnp.int32, (8, WIDE), 0)
    for bit in (4, 2, 1):
        block = jnp.where((sub & bit) == 0, pltpu.roll(block, bit, 1), block)
    return jnp.sum(block, axis=0, keepdims=True)


def kernel(
    n_dp, n_seq, n_enc, pool, slots,
    q_hbm, g_hbm, k_hbm, v_hbm, count_hbm, id_hbm, bias_hbm,
    context_out, query_out, key_out, value_out, bias_out,
    q_buf, g_buf, k_buf, v_buf, k_turn, v_turn, counts, ids, line, wide_line, bias_map,
    s_buf, d_buf, w_all, ds_all, bias_sum, c_buf, dq_buf, dk_buf, dv_buf, parts, bias_row,
    load_sem, own_sem, store_sem,
    q_send, q_recv, g_send, g_recv, c_send, c_recv, dq_send, dq_recv, b_send, b_recv,
):
    dp, seq, enc = lax.axis_index("dp"), lax.axis_index("seq"), lax.axis_index("enc")
    total = n_dp * n_seq
    flat = dp * n_seq + seq
    table = line.shape[1]

    together = 2 if n_enc % 2 == 0 else 1
    groups = n_enc // together
    paired = n_enc <= 8 and n_enc & (n_enc - 1) == 0

    def partner(step):
        place = enc
        bit = 1
        while bit < n_enc:
            if step & bit:
                place = place + bit * (1 - 2 * lax.rem(enc // bit, 2))
            bit *= 2
        return place

    def to_peer(step):
        return partner(step) if paired else lax.rem(enc + step, n_enc)

    def from_peer(step):
        return partner(step) if paired else lax.rem(enc + (n_enc - step), n_enc)

    def group_at(place):
        return (place // n_seq, lax.rem(place, n_seq), enc)

    def other(step):
        return lax.rem(flat + step, total)

    barrier = pltpu.get_barrier_semaphore()

    def greet(step):
        pl.semaphore_signal(barrier, inc=1, device_id=(dp, seq, to_peer(step)), device_id_type=MESH)

    def greet_group(step):
        pl.semaphore_signal(barrier, inc=1, device_id=group_at(other(step)), device_id_type=MESH)

    each(1, n_enc, greet)
    each(1, total, greet_group)

    loads = [
        (bias_hbm, line),
        (count_hbm, counts),
        (id_hbm, ids),
        (k_hbm, k_buf),
        (q_hbm.at[0, :, span(enc)], q_buf.at[span(0)]),
        (v_hbm, v_buf),
        (g_hbm.at[0, :, span(enc)], g_buf.at[span(0)]),
    ]
    loads = [pltpu.make_async_copy(a, b, load_sem.at[i]) for i, (a, b) in enumerate(loads)]
    for load in loads:
        load.start()
    pl.semaphore_wait(barrier, n_enc - 1 + total - 1)

    def q_copy(step):
        return pltpu.make_async_remote_copy(
            q_hbm.at[0, :, span(to_peer(step))], q_buf.at[span(step)],
            q_send.at[step], q_recv.at[step], (dp, seq, to_peer(step)), MESH,
        )

    def g_copy(step):
        return pltpu.make_async_remote_copy(
            g_hbm.at[0, :, span(to_peer(step))], g_buf.at[span(step)],
            g_send.at[step], g_recv.at[step], (dp, seq, to_peer(step)), MESH,
        )

    def c_copy(step, column):
        return pltpu.make_async_remote_copy(
            c_buf.at[span(step)], context_out.at[0, :, span(column)],
            c_send.at[step], c_recv.at[step], (dp, seq, from_peer(step)), MESH,
        )

    def dq_copy(step, column):
        return pltpu.make_async_remote_copy(
            dq_buf.at[span(step)], query_out.at[0, :, span(column)],
            dq_send.at[step], dq_recv.at[step], (dp, seq, from_peer(step)), MESH,
        )

    def b_copy(step, place):
        return pltpu.make_async_remote_copy(
            bias_row, parts.at[place],
            b_send.at[step], b_recv.at[step], group_at(other(step)), MESH,
        )

    def send_inputs(step):
        q_copy(step).start()
        g_copy(step).start()

    each(1, n_enc, lambda step: send_inputs(n_enc - step))

    for load in loads:
        load.wait()
    wide_line[...] = jnp.zeros_like(wide_line)
    wide_line[:, 0:table] = line[...]
    bias_one = spread_bias(wide_line[...])
    for at in range(together):
        bias_map[:, span(at)] = bias_one
    bias_sum[...] = jnp.zeros_like(bias_sum)
    for p in range(pool):
        k_turn[:, p * PASSAGE : (p + 1) * PASSAGE] = k_buf[p * PASSAGE : (p + 1) * PASSAGE, :].T
        v_turn[:, p * PASSAGE : (p + 1) * PASSAGE] = v_buf[p * PASSAGE : (p + 1) * PASSAGE, :].T

    def allowed(step):
        source = from_peer(step)
        lane = lax.broadcasted_iota(jnp.int32, (8, ROWS), 1)
        sub = lax.broadcasted_iota(jnp.int32, (8, ROWS), 0)
        first = lane < BLOCK_LEN
        count = jnp.where(first, counts[0, source], counts[1, source])
        mask = jnp.full((8, ROWS), NEG_FILL, F32)
        for j in range(slots):
            picked = jnp.where(first, ids[source, 0, j], ids[source, 1, j])
            mask = jnp.where((picked == sub) & (count > j), 0.0, mask)
        return mask, count

    def weigh(batch):
        at = batch * together
        here = span(at, together)
        columns = together * ROWS
        query, grad = q_buf[here, :], g_buf[here, :]
        masks = [allowed(at + k) for k in range(together)]
        mask = jnp.concatenate([pair[0] for pair in masks], axis=1)
        count = jnp.concatenate([pair[1] for pair in masks], axis=1)
        live = count[0:1, :] > 0

        def tile(p):
            return pl.ds(p * PASSAGE, PASSAGE)

        def group(x):
            return x.reshape(PASSAGE // 8, 8, columns)

        top = jnp.full((8, columns), 2 * NEG_FILL, F32)
        for p in range(pool):
            x = dot(k_buf[tile(p), :], query, 1, 1) * SCALE + bias_map[...]
            s_buf[tile(p), :] = x
            top = jnp.maximum(top, jnp.max(group(x), axis=0) + mask[p : p + 1, :])
        top = jnp.max(top, axis=0, keepdims=True)
        shift = mask - jnp.where(live, top, 0.0)
        sums = jnp.zeros((8, columns), F32)
        dots = jnp.zeros((8, columns), F32)
        for p in range(pool):
            d = dot(v_buf[tile(p), :], grad, 1, 1)
            e = jnp.exp(s_buf[tile(p), :] + shift[p : p + 1, :])
            s_buf[tile(p), :] = e
            d_buf[tile(p), :] = d
            sums = sums + jnp.sum(group(e), axis=0)
            dots = dots + jnp.sum(group(e * d), axis=0)
        sums = jnp.sum(sums, axis=0, keepdims=True)
        inverse = jnp.where(live, 1.0 / sums, 0.0)
        delta = jnp.sum(dots, axis=0, keepdims=True) * inverse
        piece = 32
        for low in range(0, PASSAGE, piece):
            bias_here = bias_sum[low : low + piece, :]
            for p in range(pool):
                rows = pl.ds(p * PASSAGE + low, piece)
                w = s_buf[rows, :] * inverse
                ds = w * (d_buf[rows, :] - delta)
                w_all[rows, here] = w.astype(BF16)
                ds_all[rows, here] = ds.astype(BF16)
                bias_here = bias_here + ds
            bias_sum[low : low + piece, :] = bias_here

    def give_back(batch):
        here = span(batch * together, together)
        c_turn = dot(v_turn[...], w_all[:, here], 1, 0)
        c_buf[here, :] = c_turn.T.astype(BF16)
        each_of(batch, lambda step: c_copy(step, enc).start())
        dq_turn = dot(k_turn[...], ds_all[:, here], 1, 0) * SCALE
        dq_buf[here, :] = dq_turn.T.astype(BF16)
        each_of(batch, lambda step: dq_copy(step, enc).start())

    def each_of(batch, body):
        for k in range(together):
            if not (isinstance(batch, int) and batch * together + k == 0):
                body(batch * together + k)

    def arrive(step):
        q_copy(step).wait_recv()
        g_copy(step).wait_recv()

    def one_batch(batch):
        each_of(batch, arrive)
        weigh(batch)
        give_back(batch)

    one_batch(0)
    own = [
        pltpu.make_async_copy(c_buf.at[span(0)], context_out.at[0, :, span(enc)], own_sem.at[0]),
        pltpu.make_async_copy(dq_buf.at[span(0)], query_out.at[0, :, span(enc)], own_sem.at[1]),
    ]
    for copy in own:
        copy.start()

    def send_bias():
        bias_row[...] = fold_bias(bias_sum[...])
        each(1, total, lambda step: b_copy(step, flat).start())

    last = groups - 1
    each(1, last, one_batch, unrolled=2)
    if last > 0:
        each_of(last, arrive)
        weigh(last)
    send_bias()
    if last > 0:
        give_back(last)

    dk_buf[...] = (dot(ds_all[...], q_buf[...], 1, 0) * SCALE).astype(BF16)
    key_store = pltpu.make_async_copy(dk_buf, key_out, store_sem.at[0])
    key_store.start()
    dv_buf[...] = dot(w_all[...], g_buf[...], 1, 0).astype(BF16)
    value_store = pltpu.make_async_copy(dv_buf, value_out, store_sem.at[1])
    value_store.start()

    parts[flat] = bias_row[...]

    def end_bias(step):
        b_copy(step, lax.rem(flat + (total - step), total)).wait_recv()

    each(1, total, end_bias)
    bias_total = parts[0]
    for place in range(1, total):
        bias_total = bias_total + parts[place]
    line[...] = bias_total[:, 0:table]
    bias_store = pltpu.make_async_copy(line, bias_out, store_sem.at[2])
    bias_store.start()

    def end_sends(step):
        q_copy(step).wait_send()
        g_copy(step).wait_send()
        c_copy(step, enc).wait_send()
        dq_copy(step, enc).wait_send()
        c_copy(step, to_peer(step)).wait_recv()
        dq_copy(step, to_peer(step)).wait_recv()

    each(1, n_enc, end_sends)
    each(1, total, lambda step: b_copy(step, flat).wait_send())
    for copy in own:
        copy.wait()
    key_store.wait()
    value_store.wait()
    bias_store.wait()


def write_out(*refs):
    sources, targets, sem = refs[:5], refs[5:10], refs[10]
    copies = [
        pltpu.make_async_copy(source, target, sem.at[i])
        for i, (source, target) in enumerate(zip(sources, targets))
    ]
    for copy in copies:
        copy.start()
    for copy in copies:
        copy.wait()


def local(n_dp, n_seq, n_enc, queries, cotangent, key_pool, value_pool, counts, neighbour_ids, rel_bias):
    pool = key_pool.shape[2]
    tokens = pool * PASSAGE
    slots = neighbour_ids.shape[-1]
    table = rel_bias.shape[1]
    total = n_dp * n_seq
    all_rows = n_enc * ROWS
    batch_rows = ROWS * (2 if n_enc % 2 == 0 else 1)
    anywhere = pl.BlockSpec(memory_space=pl.ANY)
    held = pl.BlockSpec(memory_space=pltpu.HBM)
    results = pl.pallas_call(
        functools.partial(kernel, n_dp, n_seq, n_enc, pool, slots),
        out_shape=[
            jax.ShapeDtypeStruct(queries.shape, BF16),
            jax.ShapeDtypeStruct(queries.shape, BF16),
            jax.ShapeDtypeStruct((tokens, HEAD_DIM), BF16),
            jax.ShapeDtypeStruct((tokens, HEAD_DIM), BF16),
            jax.ShapeDtypeStruct(rel_bias.shape, F32),
        ],
        in_specs=[held] * 7,
        out_specs=[anywhere] * 5,
        scratch_shapes=[
            pltpu.VMEM((all_rows, HEAD_DIM), BF16),
            pltpu.VMEM((all_rows, HEAD_DIM), BF16),
            pltpu.VMEM((tokens, HEAD_DIM), BF16),
            pltpu.VMEM((tokens, HEAD_DIM), BF16),
            pltpu.VMEM((HEAD_DIM, tokens), BF16),
            pltpu.VMEM((HEAD_DIM, tokens), BF16),
            pltpu.SMEM(counts.shape[::-1], jnp.int32),
            pltpu.SMEM(neighbour_ids.shape, jnp.int32),
            pltpu.VMEM((1, table), F32),
            pltpu.VMEM((1, WIDE), F32),
            pltpu.VMEM((PASSAGE, batch_rows), F32),
            pltpu.VMEM((tokens, batch_rows), F32),
            pltpu.VMEM((tokens, batch_rows), F32),
            pltpu.VMEM((tokens, all_rows), BF16),
            pltpu.VMEM((tokens, all_rows), BF16),
            pltpu.VMEM((PASSAGE, batch_rows), F32),
            pltpu.VMEM((all_rows, HEAD_DIM), BF16),
            pltpu.VMEM((all_rows, HEAD_DIM), BF16),
            pltpu.VMEM((tokens, HEAD_DIM), BF16),
            pltpu.VMEM((tokens, HEAD_DIM), BF16),
            pltpu.VMEM((total, 1, WIDE), F32),
            pltpu.VMEM((1, WIDE), F32),
            pltpu.SemaphoreType.DMA((7,)),
            pltpu.SemaphoreType.DMA((2,)),
            pltpu.SemaphoreType.DMA((3,)),
        ]
        + [pltpu.SemaphoreType.DMA((n_enc,))] * 8
        + [pltpu.SemaphoreType.DMA((total,))] * 2,
        compiler_params=pltpu.CompilerParams(
            collective_id=0, has_side_effects=True, vmem_limit_bytes=48 * 1024 * 1024
        ),
        name="retrieval_attention",
    )(
        pltpu.with_memory_space_constraint(queries, pltpu.HBM),
        pltpu.with_memory_space_constraint(cotangent, pltpu.HBM),
        pltpu.with_memory_space_constraint(key_pool.reshape(tokens, HEAD_DIM), pltpu.HBM),
        pltpu.with_memory_space_constraint(value_pool.reshape(tokens, HEAD_DIM), pltpu.HBM),
        pltpu.with_memory_space_constraint(counts.T, pltpu.HBM),
        pltpu.with_memory_space_constraint(neighbour_ids, pltpu.HBM),
        pltpu.with_memory_space_constraint(rel_bias, pltpu.HBM),
    )
    context, query_grad, key_grad, value_grad, bias_grad = pl.pallas_call(
        write_out,
        out_shape=[jax.ShapeDtypeStruct(x.shape, x.dtype) for x in results],
        in_specs=[anywhere] * 5,
        out_specs=[held] * 5,
        scratch_shapes=[pltpu.SemaphoreType.DMA((5,))],
        compiler_params=pltpu.CompilerParams(vmem_limit_bytes=2 * 1024 * 1024),
        name="write_out",
    )(*results)
    return (
        context,
        query_grad,
        key_grad.reshape(key_pool.shape),
        value_grad.reshape(value_pool.shape),
        bias_grad,
    )


def solution(mesh):
    in_specs = (
        P(("dp", "enc"), "seq", None),
        P(("dp", "enc"), "seq", None),
        P("dp", "seq", None, None, "enc"),
        P("dp", "seq", None, None, "enc"),
        P("dp", "seq"),
        P("dp", "seq", None),
        P("enc", None),
    )
    out_specs = (
        P(("dp", "enc"), "seq", None),
        P(("dp", "enc"), "seq", None),
        P("dp", "seq", None, None, "enc"),
        P("dp", "seq", None, None, "enc"),
        P("enc", None),
    )
    body = functools.partial(local, mesh.shape["dp"], mesh.shape["seq"], mesh.shape["enc"])
    return jax.shard_map(body, mesh=mesh, in_specs=in_specs, out_specs=out_specs, check_vma=False)
```

```python
import functools
import math

import jax
import jax.numpy as jnp
from jax import lax
from jax.experimental import pallas as pl
from jax.experimental.pallas import tpu as pltpu
from jax.sharding import PartitionSpec as P

HEAD_DIM = 128
BLOCK_LEN = 64
PASSAGE = 128
ROWS = 128
WIDE = 256

NEG_FILL = -1e30
SCALE = 1.0 / math.sqrt(HEAD_DIM)
LOG2E = math.log2(math.e)
F32 = jnp.float32
BF16 = jnp.bfloat16
MESH = pl.DeviceIdType.MESH


def each(low, high, body, unrolled=8):
    if high - low <= unrolled:
        for step in range(low, high):
            body(step)
    else:

        def one(step, carry):
            body(step)
            return carry

        lax.fori_loop(low, high, one, 0)


def span(index, width=1):
    if isinstance(index, int):
        return pl.ds(index * ROWS, width * ROWS)
    return pl.ds(pl.multiple_of(index * ROWS, ROWS), width * ROWS)


def dot(left, right, left_dim, right_dim):
    return lax.dot_general(
        left, right, (((left_dim,), (right_dim,)), ((), ())), preferred_element_type=F32
    )


def spread_bias(line):
    rows = jnp.broadcast_to(line * LOG2E, (8, WIDE))
    sub = lax.broadcasted_iota(jnp.int32, (8, WIDE), 0)
    rows = pltpu.roll(rows, WIDE - (BLOCK_LEN - 1), 1)
    for bit in (1, 2, 4):
        rows = jnp.where((sub & bit) != 0, pltpu.roll(rows, bit, 1), rows)
    groups = [rows] + [pltpu.roll(rows, 8 * k, 1) for k in range(1, BLOCK_LEN // 8)]
    block = jnp.concatenate([group[:, :PASSAGE] for group in groups], axis=0)
    return jnp.concatenate([block, block], axis=0).T


def fold_bias(total):
    parts = [total[:, at : at + ROWS] for at in range(0, total.shape[1], ROWS)]
    turned = functools.reduce(jnp.add, parts).T
    block = turned[:BLOCK_LEN] + turned[BLOCK_LEN:]
    block = jnp.concatenate([block, jnp.zeros((BLOCK_LEN, WIDE - PASSAGE), F32)], axis=1)
    for half in (32, 16, 8):
        block = pltpu.roll(block[:half], half, 1) + block[half : 2 * half]
    sub = lax.broadcasted_iota(jnp.int32, (8, WIDE), 0)
    for bit in (4, 2, 1):
        block = jnp.where((sub & bit) == 0, pltpu.roll(block, bit, 1), block)
    return jnp.sum(block, axis=0, keepdims=True)


def kernel(
    n_dp, n_seq, n_enc, pool, slots,
    q_hbm, g_hbm, k_hbm, v_hbm, count_hbm, id_hbm, bias_hbm,
    context_out, query_out, key_out, value_out, bias_out,
    q_buf, g_buf, k_buf, v_buf, k_turn, v_turn, counts, ids, line, wide_line, bias_map,
    s_buf, d_buf, w_all, ds_all, bias_sum, c_buf, dq_buf, dk_buf, dv_buf, dp_parts, seq_parts,
    load_sem, own_sem, store_sem,
    q_send, q_recv, g_send, g_recv, c_send, c_recv, dq_send, dq_recv,
    dp_send, dp_recv, seq_send, seq_recv,
):
    dp, seq, enc = lax.axis_index("dp"), lax.axis_index("seq"), lax.axis_index("enc")
    table = line.shape[1]

    together = 2 if n_enc % 2 == 0 else 1
    groups = n_enc // together
    paired = n_enc <= 8 and n_enc & (n_enc - 1) == 0

    def partner(step):
        place = enc
        bit = 1
        while bit < n_enc:
            if step & bit:
                place = place + bit * (1 - 2 * lax.rem(enc // bit, 2))
            bit *= 2
        return place

    def to_peer(step):
        return partner(step) if paired else lax.rem(enc + step, n_enc)

    def from_peer(step):
        return partner(step) if paired else lax.rem(enc + (n_enc - step), n_enc)

    def at_dp(place):
        return (place, seq, enc)

    def at_seq(place):
        return (dp, place, enc)

    barrier = pltpu.get_barrier_semaphore()

    def greet(step):
        pl.semaphore_signal(barrier, inc=1, device_id=(dp, seq, to_peer(step)), device_id_type=MESH)

    def greet_place(place):
        pl.semaphore_signal(barrier, inc=1, device_id=place, device_id_type=MESH)

    neighbours = [
        (dp > 0, at_dp(dp - 1)),
        (dp < n_dp - 1, at_dp(dp + 1)),
        (seq > 0, at_seq(seq - 1)),
        (seq < n_seq - 1, at_seq(seq + 1)),
    ]
    each(1, n_enc, greet)
    for there, place in neighbours:
        pl.when(there)(functools.partial(greet_place, place))

    loads = [
        (bias_hbm, line),
        (count_hbm, counts),
        (id_hbm, ids),
        (k_hbm, k_buf),
        (q_hbm.at[0, :, span(enc)], q_buf.at[span(0)]),
        (v_hbm, v_buf),
        (g_hbm.at[0, :, span(enc)], g_buf.at[span(0)]),
    ]
    loads = [pltpu.make_async_copy(a, b, load_sem.at[i]) for i, (a, b) in enumerate(loads)]
    for load in loads:
        load.start()
    around = 0
    for place, size in ((dp, n_dp), (seq, n_seq)):
        for distance in (place, size - 1 - place):
            around = around + (distance + size - 1) // size
    pl.semaphore_wait(barrier, n_enc - 1 + around)

    def q_copy(step):
        return pltpu.make_async_remote_copy(
            q_hbm.at[0, :, span(to_peer(step))], q_buf.at[span(step)],
            q_send.at[step], q_recv.at[step], (dp, seq, to_peer(step)), MESH,
        )

    def g_copy(step):
        return pltpu.make_async_remote_copy(
            g_hbm.at[0, :, span(to_peer(step))], g_buf.at[span(step)],
            g_send.at[step], g_recv.at[step], (dp, seq, to_peer(step)), MESH,
        )

    def c_copy(step, column):
        return pltpu.make_async_remote_copy(
            c_buf.at[span(step)], context_out.at[0, :, span(column)],
            c_send.at[step], c_recv.at[step], (dp, seq, from_peer(step)), MESH,
        )

    def dq_copy(step, column):
        return pltpu.make_async_remote_copy(
            dq_buf.at[span(step)], query_out.at[0, :, span(column)],
            dq_send.at[step], dq_recv.at[step], (dp, seq, from_peer(step)), MESH,
        )

    def line_of(place, size, at, parts, send, recv):
        def hop(side, k):
            slot = place + k if side == 0 else place - k
            target = place - 1 if side == 0 else place + 1
            return pltpu.make_async_remote_copy(
                parts.at[slot], parts.at[slot],
                send.at[side * size + k], recv.at[slot], at(target), MESH,
            )

        def has(side, k):
            return place + k < size if side == 0 else place >= k

        def onward(side):
            return place > 0 if side == 0 else place < size - 1

        def arrival(side, k):
            slot = place + k if side == 0 else place - k
            origin = place + 1 if side == 0 else place - 1
            pltpu.make_async_remote_copy(
                parts.at[slot], parts.at[slot],
                send.at[side * size + k], recv.at[slot], at(origin), MESH,
            ).wait_recv()

        def start(row):
            parts[place] = row
            for side in (0, 1):
                pl.when(onward(side))(lambda side=side: hop(side, 0).start())

        def step(k):
            for side in (0, 1):
                pl.when(has(side, k))(lambda side=side: arrival(side, k))
                pl.when(has(side, k) & onward(side))(lambda side=side: hop(side, k).start())

        def end():
            for k in range(size - 1):
                for side in (0, 1):
                    pl.when(has(side, k) & onward(side))(
                        lambda side=side, k=k: hop(side, k).wait_send()
                    )

        def added():
            return functools.reduce(jnp.add, [parts[k] for k in range(size)])

        return start, step, end, added

    dp_start, dp_step, dp_end, dp_added = line_of(dp, n_dp, at_dp, dp_parts, dp_send, dp_recv)
    seq_start, seq_step, seq_end, seq_added = line_of(
        seq, n_seq, at_seq, seq_parts, seq_send, seq_recv
    )

    def send_inputs(step):
        q_copy(step).start()
        g_copy(step).start()

    each(1, n_enc, lambda step: send_inputs(n_enc - step))

    for load in loads:
        load.wait()
    wide_line[...] = jnp.zeros_like(wide_line)
    wide_line[:, 0:table] = line[...]
    bias_one = spread_bias(wide_line[...])
    for at in range(together):
        bias_map[:, span(at)] = bias_one
    bias_sum[...] = jnp.zeros_like(bias_sum)
    for p in range(pool):
        k_turn[:, p * PASSAGE : (p + 1) * PASSAGE] = k_buf[p * PASSAGE : (p + 1) * PASSAGE, :].T
        v_turn[:, p * PASSAGE : (p + 1) * PASSAGE] = v_buf[p * PASSAGE : (p + 1) * PASSAGE, :].T

    def allowed(step):
        source = from_peer(step)
        lane = lax.broadcasted_iota(jnp.int32, (8, ROWS), 1)
        sub = lax.broadcasted_iota(jnp.int32, (8, ROWS), 0)
        first = lane < BLOCK_LEN
        count = jnp.where(first, counts[0, source], counts[1, source])
        mask = jnp.full((8, ROWS), NEG_FILL, F32)
        for j in range(slots):
            picked = jnp.where(first, ids[source, 0, j], ids[source, 1, j])
            mask = jnp.where((picked == sub) & (count > j), 0.0, mask)
        return mask, count

    def weigh(batch):
        at = batch * together
        here = span(at, together)
        columns = together * ROWS
        query, grad = q_buf[here, :], g_buf[here, :]
        masks = [allowed(at + k) for k in range(together)]
        mask = jnp.concatenate([pair[0] for pair in masks], axis=1)
        count = jnp.concatenate([pair[1] for pair in masks], axis=1)
        live = count[0:1, :] > 0

        def tile(p):
            return pl.ds(p * PASSAGE, PASSAGE)

        def group(x):
            return x.reshape(PASSAGE // 8, 8, columns)

        top = jnp.full((1, columns), 2 * NEG_FILL, F32)
        for pair in range(0, pool, 2):
            raw = dot(k_buf[pl.ds(pair * PASSAGE, 2 * PASSAGE), :], query, 1, 1)
            for p in (pair, pair + 1):
                x = raw[(p - pair) * PASSAGE : (p - pair + 1) * PASSAGE]
                x = x * (SCALE * LOG2E) + bias_map[...]
                s_buf[tile(p), :] = x
                highest = jnp.max(jnp.max(group(x), axis=0), axis=0, keepdims=True)
                top = jnp.maximum(top, highest + mask[p : p + 1, :])
        shift = mask - jnp.where(live, top, 0.0)
        sums = jnp.zeros((8, columns), F32)
        dots = jnp.zeros((8, columns), F32)
        for pair in range(0, pool, 2):
            raw = dot(v_buf[pl.ds(pair * PASSAGE, 2 * PASSAGE), :], grad, 1, 1)
            for p in (pair, pair + 1):
                d = raw[(p - pair) * PASSAGE : (p - pair + 1) * PASSAGE]
                e = jnp.exp2(s_buf[tile(p), :] + shift[p : p + 1, :])
                s_buf[tile(p), :] = e
                d_buf[tile(p), :] = d
                sums = sums + jnp.sum(group(e), axis=0)
                dots = dots + jnp.sum(group(e * d), axis=0)
        sums = jnp.sum(sums, axis=0, keepdims=True)
        inverse = jnp.where(live, 1.0 / sums, 0.0)
        delta = jnp.sum(dots, axis=0, keepdims=True) * inverse
        bias_here = bias_sum[...]
        for p in range(pool):
            w = s_buf[tile(p), :] * inverse
            ds = w * (d_buf[tile(p), :] - delta)
            w_all[tile(p), here] = w.astype(BF16)
            ds_all[tile(p), here] = ds.astype(BF16)
            bias_here = bias_here + ds
        bias_sum[...] = bias_here

    def give_back(batch):
        here = span(batch * together, together)
        c_turn = dot(v_turn[...], w_all[:, here], 1, 0)
        c_buf[here, :] = c_turn.T.astype(BF16)
        each_of(batch, lambda step: c_copy(step, enc).start())
        dq_turn = dot(k_turn[...], ds_all[:, here], 1, 0) * SCALE
        dq_buf[here, :] = dq_turn.T.astype(BF16)
        each_of(batch, lambda step: dq_copy(step, enc).start())

    def each_of(batch, body):
        for k in range(together):
            if not (isinstance(batch, int) and batch * together + k == 0):
                body(batch * together + k)

    def arrive(step):
        q_copy(step).wait_recv()
        g_copy(step).wait_recv()

    def one_batch(batch):
        each_of(batch, arrive)
        weigh(batch)
        give_back(batch)

    one_batch(0)
    own = [
        pltpu.make_async_copy(c_buf.at[span(0)], context_out.at[0, :, span(enc)], own_sem.at[0]),
        pltpu.make_async_copy(dq_buf.at[span(0)], query_out.at[0, :, span(enc)], own_sem.at[1]),
    ]
    for copy in own:
        copy.start()

    last = groups - 1
    each(1, last, one_batch, unrolled=2)
    if last > 0:
        each_of(last, arrive)
        weigh(last)
    dp_start(fold_bias(bias_sum[...]))
    if last > 0:
        give_back(last)
    for k in range(1, n_dp):
        dp_step(k)
    seq_start(dp_added())

    dk_buf[...] = (dot(ds_all[...], q_buf[...], 1, 0) * SCALE).astype(BF16)
    key_store = pltpu.make_async_copy(dk_buf, key_out, store_sem.at[0])
    key_store.start()
    dv_buf[...] = dot(w_all[...], g_buf[...], 1, 0).astype(BF16)
    value_store = pltpu.make_async_copy(dv_buf, value_out, store_sem.at[1])
    value_store.start()

    for k in range(1, n_seq):
        seq_step(k)
    bias_total = seq_added()
    line[...] = bias_total[:, 0:table]
    bias_store = pltpu.make_async_copy(line, bias_out, store_sem.at[2])
    bias_store.start()

    def end_sends(step):
        q_copy(step).wait_send()
        g_copy(step).wait_send()
        c_copy(step, enc).wait_send()
        dq_copy(step, enc).wait_send()
        c_copy(step, to_peer(step)).wait_recv()
        dq_copy(step, to_peer(step)).wait_recv()

    each(1, n_enc, end_sends)
    dp_end()
    seq_end()
    for copy in own:
        copy.wait()
    key_store.wait()
    value_store.wait()
    bias_store.wait()


def write_out(*refs):
    sources, targets, sem = refs[:5], refs[5:10], refs[10]
    copies = [
        pltpu.make_async_copy(source, target, sem.at[i])
        for i, (source, target) in enumerate(zip(sources, targets))
    ]
    for copy in copies:
        copy.start()
    for copy in copies:
        copy.wait()


def local(n_dp, n_seq, n_enc, queries, cotangent, key_pool, value_pool, counts, neighbour_ids, rel_bias):
    pool = key_pool.shape[2]
    tokens = pool * PASSAGE
    slots = neighbour_ids.shape[-1]
    table = rel_bias.shape[1]
    all_rows = n_enc * ROWS
    batch_rows = ROWS * (2 if n_enc % 2 == 0 else 1)
    anywhere = pl.BlockSpec(memory_space=pl.ANY)
    held = pl.BlockSpec(memory_space=pltpu.HBM)
    results = pl.pallas_call(
        functools.partial(kernel, n_dp, n_seq, n_enc, pool, slots),
        out_shape=[
            jax.ShapeDtypeStruct(queries.shape, BF16),
            jax.ShapeDtypeStruct(queries.shape, BF16),
            jax.ShapeDtypeStruct((tokens, HEAD_DIM), BF16),
            jax.ShapeDtypeStruct((tokens, HEAD_DIM), BF16),
            jax.ShapeDtypeStruct(rel_bias.shape, F32),
        ],
        in_specs=[held] * 7,
        out_specs=[anywhere] * 5,
        scratch_shapes=[
            pltpu.VMEM((all_rows, HEAD_DIM), BF16),
            pltpu.VMEM((all_rows, HEAD_DIM), BF16),
            pltpu.VMEM((tokens, HEAD_DIM), BF16),
            pltpu.VMEM((tokens, HEAD_DIM), BF16),
            pltpu.VMEM((HEAD_DIM, tokens), BF16),
            pltpu.VMEM((HEAD_DIM, tokens), BF16),
            pltpu.SMEM(counts.shape[::-1], jnp.int32),
            pltpu.SMEM(neighbour_ids.shape, jnp.int32),
            pltpu.VMEM((1, table), F32),
            pltpu.VMEM((1, WIDE), F32),
            pltpu.VMEM((PASSAGE, batch_rows), F32),
            pltpu.VMEM((tokens, batch_rows), F32),
            pltpu.VMEM((tokens, batch_rows), F32),
            pltpu.VMEM((tokens, all_rows), BF16),
            pltpu.VMEM((tokens, all_rows), BF16),
            pltpu.VMEM((PASSAGE, batch_rows), F32),
            pltpu.VMEM((all_rows, HEAD_DIM), BF16),
            pltpu.VMEM((all_rows, HEAD_DIM), BF16),
            pltpu.VMEM((tokens, HEAD_DIM), BF16),
            pltpu.VMEM((tokens, HEAD_DIM), BF16),
            pltpu.VMEM((n_dp, 1, WIDE), F32),
            pltpu.VMEM((n_seq, 1, WIDE), F32),
            pltpu.SemaphoreType.DMA((7,)),
            pltpu.SemaphoreType.DMA((2,)),
            pltpu.SemaphoreType.DMA((3,)),
        ]
        + [pltpu.SemaphoreType.DMA((n_enc,))] * 8
        + [
            pltpu.SemaphoreType.DMA((2 * n_dp,)),
            pltpu.SemaphoreType.DMA((n_dp,)),
            pltpu.SemaphoreType.DMA((2 * n_seq,)),
            pltpu.SemaphoreType.DMA((n_seq,)),
        ],
        compiler_params=pltpu.CompilerParams(
            collective_id=0, has_side_effects=True, vmem_limit_bytes=48 * 1024 * 1024
        ),
        name="retrieval_attention",
    )(
        pltpu.with_memory_space_constraint(queries, pltpu.HBM),
        pltpu.with_memory_space_constraint(cotangent, pltpu.HBM),
        pltpu.with_memory_space_constraint(key_pool.reshape(tokens, HEAD_DIM), pltpu.HBM),
        pltpu.with_memory_space_constraint(value_pool.reshape(tokens, HEAD_DIM), pltpu.HBM),
        pltpu.with_memory_space_constraint(counts.T, pltpu.HBM),
        pltpu.with_memory_space_constraint(neighbour_ids, pltpu.HBM),
        pltpu.with_memory_space_constraint(rel_bias, pltpu.HBM),
    )
    context, query_grad, key_grad, value_grad, bias_grad = pl.pallas_call(
        write_out,
        out_shape=[jax.ShapeDtypeStruct(x.shape, x.dtype) for x in results],
        in_specs=[anywhere] * 5,
        out_specs=[held] * 5,
        scratch_shapes=[pltpu.SemaphoreType.DMA((5,))],
        compiler_params=pltpu.CompilerParams(vmem_limit_bytes=2 * 1024 * 1024),
        name="write_out",
    )(*results)
    return (
        context,
        query_grad,
        key_grad.reshape(key_pool.shape),
        value_grad.reshape(value_pool.shape),
        bias_grad,
    )


def solution(mesh):
    in_specs = (
        P(("dp", "enc"), "seq", None),
        P(("dp", "enc"), "seq", None),
        P("dp", "seq", None, None, "enc"),
        P("dp", "seq", None, None, "enc"),
        P("dp", "seq"),
        P("dp", "seq", None),
        P("enc", None),
    )
    out_specs = (
        P(("dp", "enc"), "seq", None),
        P(("dp", "enc"), "seq", None),
        P("dp", "seq", None, None, "enc"),
        P("dp", "seq", None, None, "enc"),
        P("enc", None),
    )
    body = functools.partial(local, mesh.shape["dp"], mesh.shape["seq"], mesh.shape["enc"])
    return jax.shard_map(body, mesh=mesh, in_specs=in_specs, out_specs=out_specs, check_vma=False)
```

```python
import functools
import math

import jax
import jax.numpy as jnp
from jax import lax
from jax.experimental import pallas as pl
from jax.experimental.pallas import tpu as pltpu
from jax.sharding import PartitionSpec as P

HEAD_DIM = 128
BLOCK_LEN = 64
PASSAGE = 128
ROWS = 128
WIDE = 256

NEG_FILL = -1e30
SCALE = 1.0 / math.sqrt(HEAD_DIM)
LOG2E = math.log2(math.e)
F32 = jnp.float32
BF16 = jnp.bfloat16
MESH = pl.DeviceIdType.MESH


def each(low, high, body, unrolled=8):
    if high - low <= unrolled:
        for step in range(low, high):
            body(step)
    else:

        def one(step, carry):
            body(step)
            return carry

        lax.fori_loop(low, high, one, 0)


def span(index, width=1):
    if isinstance(index, int):
        return pl.ds(index * ROWS, width * ROWS)
    return pl.ds(pl.multiple_of(index * ROWS, ROWS), width * ROWS)


def dot(left, right, left_dim, right_dim):
    return lax.dot_general(
        left, right, (((left_dim,), (right_dim,)), ((), ())), preferred_element_type=F32
    )


def spread_bias(line):
    rows = jnp.broadcast_to(line * LOG2E, (8, WIDE))
    sub = lax.broadcasted_iota(jnp.int32, (8, WIDE), 0)
    rows = pltpu.roll(rows, WIDE - (BLOCK_LEN - 1), 1)
    for bit in (1, 2, 4):
        rows = jnp.where((sub & bit) != 0, pltpu.roll(rows, bit, 1), rows)
    groups = [rows] + [pltpu.roll(rows, 8 * k, 1) for k in range(1, BLOCK_LEN // 8)]
    block = jnp.concatenate([group[:, :PASSAGE] for group in groups], axis=0)
    return jnp.concatenate([block, block], axis=0).T


def fold_bias(total):
    parts = [total[:, at : at + ROWS] for at in range(0, total.shape[1], ROWS)]
    turned = functools.reduce(jnp.add, parts).T
    block = turned[:BLOCK_LEN] + turned[BLOCK_LEN:]
    block = jnp.concatenate([block, jnp.zeros((BLOCK_LEN, WIDE - PASSAGE), F32)], axis=1)
    for half in (32, 16, 8):
        block = pltpu.roll(block[:half], half, 1) + block[half : 2 * half]
    sub = lax.broadcasted_iota(jnp.int32, (8, WIDE), 0)
    for bit in (4, 2, 1):
        block = jnp.where((sub & bit) == 0, pltpu.roll(block, bit, 1), block)
    return jnp.sum(block, axis=0, keepdims=True)


def kernel(
    n_dp, n_seq, n_enc, pool, slots,
    q_hbm, g_hbm, k_hbm, v_hbm, count_hbm, id_hbm, bias_hbm,
    context_out, query_out, key_out, value_out, bias_out,
    q_buf, g_buf, k_buf, v_buf, k_turn, v_turn, counts, ids, line, wide_line, bias_map,
    s_buf, d_buf, w_all, ds_all, bias_sum, c_buf, dq_buf, dk_buf, dv_buf, parts, bias_row,
    load_sem, own_sem, store_sem,
    q_send, q_recv, g_send, g_recv, c_send, c_recv, dq_send, dq_recv, b_send, b_recv,
):
    dp, seq, enc = lax.axis_index("dp"), lax.axis_index("seq"), lax.axis_index("enc")
    total = n_dp * n_seq
    flat = dp * n_seq + seq
    table = line.shape[1]

    together = 2 if n_enc % 2 == 0 else 1
    groups = n_enc // together
    paired = n_enc <= 8 and n_enc & (n_enc - 1) == 0

    def partner(step):
        place = enc
        bit = 1
        while bit < n_enc:
            if step & bit:
                place = place + bit * (1 - 2 * lax.rem(enc // bit, 2))
            bit *= 2
        return place

    def to_peer(step):
        return partner(step) if paired else lax.rem(enc + step, n_enc)

    def from_peer(step):
        return partner(step) if paired else lax.rem(enc + (n_enc - step), n_enc)

    def group_at(place):
        return (place // n_seq, lax.rem(place, n_seq), enc)

    def other(step):
        return lax.rem(flat + step, total)

    barrier = pltpu.get_barrier_semaphore()

    def greet(step):
        pl.semaphore_signal(barrier, inc=1, device_id=(dp, seq, to_peer(step)), device_id_type=MESH)

    def greet_group(step):
        pl.semaphore_signal(barrier, inc=1, device_id=group_at(other(step)), device_id_type=MESH)

    each(1, n_enc, greet)
    each(1, total, greet_group)

    loads = [
        (bias_hbm, line),
        (count_hbm, counts),
        (id_hbm, ids),
        (k_hbm, k_buf),
        (q_hbm.at[0, :, span(enc)], q_buf.at[span(0)]),
        (v_hbm, v_buf),
        (g_hbm.at[0, :, span(enc)], g_buf.at[span(0)]),
    ]
    loads = [pltpu.make_async_copy(a, b, load_sem.at[i]) for i, (a, b) in enumerate(loads)]
    for load in loads:
        load.start()
    pl.semaphore_wait(barrier, n_enc - 1 + total - 1)

    def q_copy(step):
        return pltpu.make_async_remote_copy(
            q_hbm.at[0, :, span(to_peer(step))], q_buf.at[span(step)],
            q_send.at[step], q_recv.at[step], (dp, seq, to_peer(step)), MESH,
        )

    def g_copy(step):
        return pltpu.make_async_remote_copy(
            g_hbm.at[0, :, span(to_peer(step))], g_buf.at[span(step)],
            g_send.at[step], g_recv.at[step], (dp, seq, to_peer(step)), MESH,
        )

    def c_copy(step, column):
        return pltpu.make_async_remote_copy(
            c_buf.at[span(step)], context_out.at[0, :, span(column)],
            c_send.at[step], c_recv.at[step], (dp, seq, from_peer(step)), MESH,
        )

    def dq_copy(step, column):
        return pltpu.make_async_remote_copy(
            dq_buf.at[span(step)], query_out.at[0, :, span(column)],
            dq_send.at[step], dq_recv.at[step], (dp, seq, from_peer(step)), MESH,
        )

    def b_copy(step, place):
        return pltpu.make_async_remote_copy(
            bias_row, parts.at[place],
            b_send.at[step], b_recv.at[step], group_at(other(step)), MESH,
        )

    def send_inputs(step):
        q_copy(step).start()
        g_copy(step).start()

    each(1, n_enc, lambda step: send_inputs(n_enc - step))

    for load in loads:
        load.wait()
    wide_line[...] = jnp.zeros_like(wide_line)
    wide_line[:, 0:table] = line[...]
    bias_one = spread_bias(wide_line[...])
    for at in range(together):
        bias_map[:, span(at)] = bias_one
    bias_sum[...] = jnp.zeros_like(bias_sum)
    for p in range(pool):
        k_turn[:, p * PASSAGE : (p + 1) * PASSAGE] = k_buf[p * PASSAGE : (p + 1) * PASSAGE, :].T
        v_turn[:, p * PASSAGE : (p + 1) * PASSAGE] = v_buf[p * PASSAGE : (p + 1) * PASSAGE, :].T

    def allowed(step):
        source = from_peer(step)
        lane = lax.broadcasted_iota(jnp.int32, (8, ROWS), 1)
        sub = lax.broadcasted_iota(jnp.int32, (8, ROWS), 0)
        first = lane < BLOCK_LEN
        count = jnp.where(first, counts[0, source], counts[1, source])
        mask = jnp.full((8, ROWS), NEG_FILL, F32)
        for j in range(slots):
            picked = jnp.where(first, ids[source, 0, j], ids[source, 1, j])
            mask = jnp.where((picked == sub) & (count > j), 0.0, mask)
        return mask, count

    def weigh(batch):
        at = batch * together
        here = span(at, together)
        columns = together * ROWS
        query, grad = q_buf[here, :], g_buf[here, :]
        masks = [allowed(at + k) for k in range(together)]
        mask = jnp.concatenate([pair[0] for pair in masks], axis=1)
        count = jnp.concatenate([pair[1] for pair in masks], axis=1)
        live = count[0:1, :] > 0

        def tile(p):
            return pl.ds(p * PASSAGE, PASSAGE)

        def group(x):
            return x.reshape(PASSAGE // 8, 8, columns)

        top = jnp.full((1, columns), 2 * NEG_FILL, F32)
        for pair in range(0, pool, 2):
            raw = dot(k_buf[pl.ds(pair * PASSAGE, 2 * PASSAGE), :], query, 1, 1)
            for p in (pair, pair + 1):
                x = raw[(p - pair) * PASSAGE : (p - pair + 1) * PASSAGE]
                x = x * (SCALE * LOG2E) + bias_map[...]
                s_buf[tile(p), :] = x
                highest = jnp.max(jnp.max(group(x), axis=0), axis=0, keepdims=True)
                top = jnp.maximum(top, highest + mask[p : p + 1, :])
        shift = mask - jnp.where(live, top, 0.0)
        sums = jnp.zeros((8, columns), F32)
        dots = jnp.zeros((8, columns), F32)
        for pair in range(0, pool, 2):
            raw = dot(v_buf[pl.ds(pair * PASSAGE, 2 * PASSAGE), :], grad, 1, 1)
            for p in (pair, pair + 1):
                d = raw[(p - pair) * PASSAGE : (p - pair + 1) * PASSAGE]
                e = jnp.exp2(s_buf[tile(p), :] + shift[p : p + 1, :])
                s_buf[tile(p), :] = e
                d_buf[tile(p), :] = d
                sums = sums + jnp.sum(group(e), axis=0)
                dots = dots + jnp.sum(group(e * d), axis=0)
        sums = jnp.sum(sums, axis=0, keepdims=True)
        inverse = jnp.where(live, 1.0 / sums, 0.0)
        delta = jnp.sum(dots, axis=0, keepdims=True) * inverse
        bias_here = bias_sum[...]
        for p in range(pool):
            w = s_buf[tile(p), :] * inverse
            ds = w * (d_buf[tile(p), :] - delta)
            w_all[tile(p), here] = w.astype(BF16)
            ds_all[tile(p), here] = ds.astype(BF16)
            bias_here = bias_here + ds
        bias_sum[...] = bias_here

    def give_back(batch):
        here = span(batch * together, together)
        c_turn = dot(v_turn[...], w_all[:, here], 1, 0)
        c_buf[here, :] = c_turn.T.astype(BF16)
        each_of(batch, lambda step: c_copy(step, enc).start())
        dq_turn = dot(k_turn[...], ds_all[:, here], 1, 0) * SCALE
        dq_buf[here, :] = dq_turn.T.astype(BF16)
        each_of(batch, lambda step: dq_copy(step, enc).start())

    def each_of(batch, body):
        for k in range(together):
            if not (isinstance(batch, int) and batch * together + k == 0):
                body(batch * together + k)

    def arrive(step):
        q_copy(step).wait_recv()
        g_copy(step).wait_recv()

    def one_batch(batch):
        each_of(batch, arrive)
        weigh(batch)
        give_back(batch)

    each_of(0, arrive)
    weigh(0)

    def send_bias():
        bias_row[...] = fold_bias(bias_sum[...])
        each(1, total, lambda step: b_copy(step, flat).start())

    last = groups - 1
    each(1, last, one_batch, unrolled=2)
    if last > 0:
        each_of(last, arrive)
        weigh(last)
    send_bias()
    give_back(0)
    own = [
        pltpu.make_async_copy(c_buf.at[span(0)], context_out.at[0, :, span(enc)], own_sem.at[0]),
        pltpu.make_async_copy(dq_buf.at[span(0)], query_out.at[0, :, span(enc)], own_sem.at[1]),
    ]
    for copy in own:
        copy.start()
    if last > 0:
        give_back(last)

    dk_buf[...] = (dot(ds_all[...], q_buf[...], 1, 0) * SCALE).astype(BF16)
    key_store = pltpu.make_async_copy(dk_buf, key_out, store_sem.at[0])
    key_store.start()
    dv_buf[...] = dot(w_all[...], g_buf[...], 1, 0).astype(BF16)
    value_store = pltpu.make_async_copy(dv_buf, value_out, store_sem.at[1])
    value_store.start()

    parts[flat] = bias_row[...]

    def end_bias(step):
        b_copy(step, lax.rem(flat + (total - step), total)).wait_recv()

    each(1, total, end_bias)
    bias_total = parts[0]
    for place in range(1, total):
        bias_total = bias_total + parts[place]
    line[...] = bias_total[:, 0:table]
    bias_store = pltpu.make_async_copy(line, bias_out, store_sem.at[2])
    bias_store.start()

    def end_sends(step):
        q_copy(step).wait_send()
        g_copy(step).wait_send()
        c_copy(step, enc).wait_send()
        dq_copy(step, enc).wait_send()
        c_copy(step, to_peer(step)).wait_recv()
        dq_copy(step, to_peer(step)).wait_recv()

    each(1, n_enc, end_sends)
    each(1, total, lambda step: b_copy(step, flat).wait_send())
    for copy in own:
        copy.wait()
    key_store.wait()
    value_store.wait()
    bias_store.wait()


def write_out(*refs):
    sources, targets, sem = refs[:5], refs[5:10], refs[10]
    copies = [
        pltpu.make_async_copy(source, target, sem.at[i])
        for i, (source, target) in enumerate(zip(sources, targets))
    ]
    for copy in copies:
        copy.start()
    for copy in copies:
        copy.wait()


def local(n_dp, n_seq, n_enc, queries, cotangent, key_pool, value_pool, counts, neighbour_ids, rel_bias):
    pool = key_pool.shape[2]
    tokens = pool * PASSAGE
    slots = neighbour_ids.shape[-1]
    table = rel_bias.shape[1]
    total = n_dp * n_seq
    all_rows = n_enc * ROWS
    batch_rows = ROWS * (2 if n_enc % 2 == 0 else 1)
    anywhere = pl.BlockSpec(memory_space=pl.ANY)
    held = pl.BlockSpec(memory_space=pltpu.HBM)
    results = pl.pallas_call(
        functools.partial(kernel, n_dp, n_seq, n_enc, pool, slots),
        out_shape=[
            jax.ShapeDtypeStruct(queries.shape, BF16),
            jax.ShapeDtypeStruct(queries.shape, BF16),
            jax.ShapeDtypeStruct((tokens, HEAD_DIM), BF16),
            jax.ShapeDtypeStruct((tokens, HEAD_DIM), BF16),
            jax.ShapeDtypeStruct(rel_bias.shape, F32),
        ],
        in_specs=[held] * 7,
        out_specs=[anywhere] * 5,
        scratch_shapes=[
            pltpu.VMEM((all_rows, HEAD_DIM), BF16),
            pltpu.VMEM((all_rows, HEAD_DIM), BF16),
            pltpu.VMEM((tokens, HEAD_DIM), BF16),
            pltpu.VMEM((tokens, HEAD_DIM), BF16),
            pltpu.VMEM((HEAD_DIM, tokens), BF16),
            pltpu.VMEM((HEAD_DIM, tokens), BF16),
            pltpu.SMEM(counts.shape[::-1], jnp.int32),
            pltpu.SMEM(neighbour_ids.shape, jnp.int32),
            pltpu.VMEM((1, table), F32),
            pltpu.VMEM((1, WIDE), F32),
            pltpu.VMEM((PASSAGE, batch_rows), F32),
            pltpu.VMEM((tokens, batch_rows), F32),
            pltpu.VMEM((tokens, batch_rows), F32),
            pltpu.VMEM((tokens, all_rows), BF16),
            pltpu.VMEM((tokens, all_rows), BF16),
            pltpu.VMEM((PASSAGE, batch_rows), F32),
            pltpu.VMEM((all_rows, HEAD_DIM), BF16),
            pltpu.VMEM((all_rows, HEAD_DIM), BF16),
            pltpu.VMEM((tokens, HEAD_DIM), BF16),
            pltpu.VMEM((tokens, HEAD_DIM), BF16),
            pltpu.VMEM((total, 1, WIDE), F32),
            pltpu.VMEM((1, WIDE), F32),
            pltpu.SemaphoreType.DMA((7,)),
            pltpu.SemaphoreType.DMA((2,)),
            pltpu.SemaphoreType.DMA((3,)),
        ]
        + [pltpu.SemaphoreType.DMA((n_enc,))] * 8
        + [pltpu.SemaphoreType.DMA((total,))] * 2,
        compiler_params=pltpu.CompilerParams(
            collective_id=0, has_side_effects=True, vmem_limit_bytes=48 * 1024 * 1024
        ),
        name="retrieval_attention",
    )(
        pltpu.with_memory_space_constraint(queries, pltpu.HBM),
        pltpu.with_memory_space_constraint(cotangent, pltpu.HBM),
        pltpu.with_memory_space_constraint(key_pool.reshape(tokens, HEAD_DIM), pltpu.HBM),
        pltpu.with_memory_space_constraint(value_pool.reshape(tokens, HEAD_DIM), pltpu.HBM),
        pltpu.with_memory_space_constraint(counts.T, pltpu.HBM),
        pltpu.with_memory_space_constraint(neighbour_ids, pltpu.HBM),
        pltpu.with_memory_space_constraint(rel_bias, pltpu.HBM),
    )
    context, query_grad, key_grad, value_grad, bias_grad = pl.pallas_call(
        write_out,
        out_shape=[jax.ShapeDtypeStruct(x.shape, x.dtype) for x in results],
        in_specs=[anywhere] * 5,
        out_specs=[held] * 5,
        scratch_shapes=[pltpu.SemaphoreType.DMA((5,))],
        compiler_params=pltpu.CompilerParams(vmem_limit_bytes=2 * 1024 * 1024),
        name="write_out",
    )(*results)
    return (
        context,
        query_grad,
        key_grad.reshape(key_pool.shape),
        value_grad.reshape(value_pool.shape),
        bias_grad,
    )


def solution(mesh):
    in_specs = (
        P(("dp", "enc"), "seq", None),
        P(("dp", "enc"), "seq", None),
        P("dp", "seq", None, None, "enc"),
        P("dp", "seq", None, None, "enc"),
        P("dp", "seq"),
        P("dp", "seq", None),
        P("enc", None),
    )
    out_specs = (
        P(("dp", "enc"), "seq", None),
        P(("dp", "enc"), "seq", None),
        P("dp", "seq", None, None, "enc"),
        P("dp", "seq", None, None, "enc"),
        P("enc", None),
    )
    body = functools.partial(local, mesh.shape["dp"], mesh.shape["seq"], mesh.shape["enc"])
    return jax.shard_map(body, mesh=mesh, in_specs=in_specs, out_specs=out_specs, check_vma=False)
```

```python
import functools
import math

import jax
import jax.numpy as jnp
from jax import lax
from jax.experimental import pallas as pl
from jax.experimental.pallas import tpu as pltpu
from jax.sharding import PartitionSpec as P

HEAD_DIM = 128
BLOCK_LEN = 64
PASSAGE = 128
ROWS = 128
WIDE = 256

NEG_FILL = -1e30
SCALE = 1.0 / math.sqrt(HEAD_DIM)
LOG2E = math.log2(math.e)
F32 = jnp.float32
BF16 = jnp.bfloat16
MESH = pl.DeviceIdType.MESH


def each(low, high, body, unrolled=8):
    if high - low <= unrolled:
        for step in range(low, high):
            body(step)
    else:

        def one(step, carry):
            body(step)
            return carry

        lax.fori_loop(low, high, one, 0)


def span(index, width=1):
    if isinstance(index, int):
        return pl.ds(index * ROWS, width * ROWS)
    return pl.ds(pl.multiple_of(index * ROWS, ROWS), width * ROWS)


def dot(left, right, left_dim, right_dim):
    return lax.dot_general(
        left, right, (((left_dim,), (right_dim,)), ((), ())), preferred_element_type=F32
    )


def spread_bias(line):
    rows = jnp.broadcast_to(line * LOG2E, (8, WIDE))
    sub = lax.broadcasted_iota(jnp.int32, (8, WIDE), 0)
    rows = pltpu.roll(rows, WIDE - (BLOCK_LEN - 1), 1)
    for bit in (1, 2, 4):
        rows = jnp.where((sub & bit) != 0, pltpu.roll(rows, bit, 1), rows)
    groups = [rows] + [pltpu.roll(rows, 8 * k, 1) for k in range(1, BLOCK_LEN // 8)]
    block = jnp.concatenate([group[:, :PASSAGE] for group in groups], axis=0)
    return jnp.concatenate([block, block], axis=0).T


def fold_bias(total):
    parts = [total[:, at : at + ROWS] for at in range(0, total.shape[1], ROWS)]
    turned = functools.reduce(jnp.add, parts).T
    block = turned[:BLOCK_LEN] + turned[BLOCK_LEN:]
    block = jnp.concatenate([block, jnp.zeros((BLOCK_LEN, WIDE - PASSAGE), F32)], axis=1)
    for half in (32, 16, 8):
        block = pltpu.roll(block[:half], half, 1) + block[half : 2 * half]
    sub = lax.broadcasted_iota(jnp.int32, (8, WIDE), 0)
    for bit in (4, 2, 1):
        block = jnp.where((sub & bit) == 0, pltpu.roll(block, bit, 1), block)
    return jnp.sum(block, axis=0, keepdims=True)


def kernel(
    n_dp, n_seq, n_enc, pool, slots,
    q_hbm, g_hbm, k_hbm, v_hbm, count_hbm, id_hbm, bias_hbm,
    context_out, query_out, key_out, value_out, bias_out,
    q_buf, g_buf, k_buf, v_buf, k_turn, v_turn, counts, ids, line, wide_line, bias_map,
    s_buf, d_buf, w_all, ds_all, bias_sum, c_buf, dq_buf, dk_buf, dv_buf, parts, bias_row,
    load_sem, own_sem, store_sem,
    q_send, q_recv, g_send, g_recv, c_send, c_recv, dq_send, dq_recv, b_send, b_recv,
):
    dp, seq, enc = lax.axis_index("dp"), lax.axis_index("seq"), lax.axis_index("enc")
    total = n_dp * n_seq
    flat = dp * n_seq + seq
    table = line.shape[1]

    together = 2 if n_enc % 2 == 0 else 1
    groups = n_enc // together
    paired = n_enc <= 8 and n_enc & (n_enc - 1) == 0

    def partner(step):
        place = enc
        bit = 1
        while bit < n_enc:
            if step & bit:
                place = place + bit * (1 - 2 * lax.rem(enc // bit, 2))
            bit *= 2
        return place

    def to_peer(step):
        return partner(step) if paired else lax.rem(enc + step, n_enc)

    def from_peer(step):
        return partner(step) if paired else lax.rem(enc + (n_enc - step), n_enc)

    def group_at(place):
        return (place // n_seq, lax.rem(place, n_seq), enc)

    def other(step):
        return lax.rem(flat + step, total)

    barrier = pltpu.get_barrier_semaphore()

    def greet(step):
        pl.semaphore_signal(barrier, inc=1, device_id=(dp, seq, to_peer(step)), device_id_type=MESH)

    def greet_group(step):
        pl.semaphore_signal(barrier, inc=1, device_id=group_at(other(step)), device_id_type=MESH)

    each(1, n_enc, greet)
    each(1, total, greet_group)

    loads = [
        (bias_hbm, line),
        (count_hbm, counts),
        (id_hbm, ids),
        (k_hbm, k_buf),
        (q_hbm.at[0, :, span(enc)], q_buf.at[span(0)]),
        (v_hbm, v_buf),
        (g_hbm.at[0, :, span(enc)], g_buf.at[span(0)]),
    ]
    loads = [pltpu.make_async_copy(a, b, load_sem.at[i]) for i, (a, b) in enumerate(loads)]
    for load in loads:
        load.start()
    pl.semaphore_wait(barrier, n_enc - 1 + total - 1)

    def q_copy(step):
        return pltpu.make_async_remote_copy(
            q_hbm.at[0, :, span(to_peer(step))], q_buf.at[span(step)],
            q_send.at[step], q_recv.at[step], (dp, seq, to_peer(step)), MESH,
        )

    def g_copy(step):
        return pltpu.make_async_remote_copy(
            g_hbm.at[0, :, span(to_peer(step))], g_buf.at[span(step)],
            g_send.at[step], g_recv.at[step], (dp, seq, to_peer(step)), MESH,
        )

    def c_copy(step, column):
        return pltpu.make_async_remote_copy(
            c_buf.at[span(step)], context_out.at[0, :, span(column)],
            c_send.at[step], c_recv.at[step], (dp, seq, from_peer(step)), MESH,
        )

    def dq_copy(step, column):
        return pltpu.make_async_remote_copy(
            dq_buf.at[span(step)], query_out.at[0, :, span(column)],
            dq_send.at[step], dq_recv.at[step], (dp, seq, from_peer(step)), MESH,
        )

    def b_copy(step, place):
        return pltpu.make_async_remote_copy(
            bias_row, parts.at[place],
            b_send.at[step], b_recv.at[step], group_at(other(step)), MESH,
        )

    def send_inputs(step):
        q_copy(step).start()
        g_copy(step).start()

    each(1, n_enc, lambda step: send_inputs(n_enc - step))

    for load in loads[:3]:
        load.wait()
    wide_line[...] = jnp.zeros_like(wide_line)
    wide_line[:, 0:table] = line[...]
    bias_one = spread_bias(wide_line[...])
    for at in range(together):
        bias_map[:, span(at)] = bias_one
    bias_sum[...] = jnp.zeros_like(bias_sum)
    for load in loads[3:]:
        load.wait()
    for p in range(pool):
        k_turn[:, p * PASSAGE : (p + 1) * PASSAGE] = k_buf[p * PASSAGE : (p + 1) * PASSAGE, :].T
        v_turn[:, p * PASSAGE : (p + 1) * PASSAGE] = v_buf[p * PASSAGE : (p + 1) * PASSAGE, :].T

    def allowed(step):
        source = from_peer(step)
        lane = lax.broadcasted_iota(jnp.int32, (8, ROWS), 1)
        sub = lax.broadcasted_iota(jnp.int32, (8, ROWS), 0)
        first = lane < BLOCK_LEN
        count = jnp.where(first, counts[0, source], counts[1, source])
        mask = jnp.full((8, ROWS), NEG_FILL, F32)
        for j in range(slots):
            picked = jnp.where(first, ids[source, 0, j], ids[source, 1, j])
            mask = jnp.where((picked == sub) & (count > j), 0.0, mask)
        return mask, count

    def weigh(batch):
        at = batch * together
        here = span(at, together)
        columns = together * ROWS
        query, grad = q_buf[here, :], g_buf[here, :]
        masks = [allowed(at + k) for k in range(together)]
        mask = jnp.concatenate([pair[0] for pair in masks], axis=1)
        count = jnp.concatenate([pair[1] for pair in masks], axis=1)
        live = count[0:1, :] > 0

        def tile(p):
            return pl.ds(p * PASSAGE, PASSAGE)

        def group(x):
            return x.reshape(PASSAGE // 8, 8, columns)

        top = jnp.full((1, columns), 2 * NEG_FILL, F32)
        for pair in range(0, pool, 2):
            raw = dot(k_buf[pl.ds(pair * PASSAGE, 2 * PASSAGE), :], query, 1, 1)
            for p in (pair, pair + 1):
                x = raw[(p - pair) * PASSAGE : (p - pair + 1) * PASSAGE]
                x = x * (SCALE * LOG2E) + bias_map[...]
                s_buf[tile(p), :] = x
                highest = jnp.max(jnp.max(group(x), axis=0), axis=0, keepdims=True)
                top = jnp.maximum(top, highest + mask[p : p + 1, :])
        shift = mask - jnp.where(live, top, 0.0)
        sums = jnp.zeros((8, columns), F32)
        dots = jnp.zeros((8, columns), F32)
        for pair in range(0, pool, 2):
            raw = dot(v_buf[pl.ds(pair * PASSAGE, 2 * PASSAGE), :], grad, 1, 1)
            for p in (pair, pair + 1):
                d = raw[(p - pair) * PASSAGE : (p - pair + 1) * PASSAGE]
                e = jnp.exp2(s_buf[tile(p), :] + shift[p : p + 1, :])
                s_buf[tile(p), :] = e
                d_buf[tile(p), :] = d
                sums = sums + jnp.sum(group(e), axis=0)
                dots = dots + jnp.sum(group(e * d), axis=0)
        sums = jnp.sum(sums, axis=0, keepdims=True)
        inverse = jnp.where(live, 1.0 / sums, 0.0)
        delta = jnp.sum(dots, axis=0, keepdims=True) * inverse
        bias_here = bias_sum[...]
        for p in range(pool):
            w = s_buf[tile(p), :] * inverse
            ds = w * (d_buf[tile(p), :] - delta)
            w_all[tile(p), here] = w.astype(BF16)
            ds_all[tile(p), here] = ds.astype(BF16)
            bias_here = bias_here + ds
        bias_sum[...] = bias_here

    def give_back(batch):
        here = span(batch * together, together)
        c_turn = dot(v_turn[...], w_all[:, here], 1, 0)
        c_buf[here, :] = c_turn.T.astype(BF16)
        each_of(batch, lambda step: c_copy(step, enc).start())
        dq_turn = dot(k_turn[...], ds_all[:, here], 1, 0) * SCALE
        dq_buf[here, :] = dq_turn.T.astype(BF16)
        each_of(batch, lambda step: dq_copy(step, enc).start())

    def each_of(batch, body):
        for k in range(together):
            if not (isinstance(batch, int) and batch * together + k == 0):
                body(batch * together + k)

    def arrive(step):
        q_copy(step).wait_recv()
        g_copy(step).wait_recv()

    def one_batch(batch):
        each_of(batch, arrive)
        weigh(batch)
        give_back(batch)

    one_batch(0)
    own = [
        pltpu.make_async_copy(c_buf.at[span(0)], context_out.at[0, :, span(enc)], own_sem.at[0]),
        pltpu.make_async_copy(dq_buf.at[span(0)], query_out.at[0, :, span(enc)], own_sem.at[1]),
    ]
    for copy in own:
        copy.start()

    def send_bias():
        bias_row[...] = fold_bias(bias_sum[...])
        each(1, total, lambda step: b_copy(step, flat).start())

    last = groups - 1
    each(1, last, one_batch, unrolled=2)
    if last > 0:
        each_of(last, arrive)
        weigh(last)
    send_bias()
    if last > 0:
        give_back(last)

    dk_buf[...] = (dot(ds_all[...], q_buf[...], 1, 0) * SCALE).astype(BF16)
    key_store = pltpu.make_async_copy(dk_buf, key_out, store_sem.at[0])
    key_store.start()
    dv_buf[...] = dot(w_all[...], g_buf[...], 1, 0).astype(BF16)
    value_store = pltpu.make_async_copy(dv_buf, value_out, store_sem.at[1])
    value_store.start()

    parts[flat] = bias_row[...]

    def end_bias(step):
        b_copy(step, lax.rem(flat + (total - step), total)).wait_recv()

    each(1, total, end_bias)
    bias_total = parts[0]
    for place in range(1, total):
        bias_total = bias_total + parts[place]
    line[...] = bias_total[:, 0:table]
    bias_store = pltpu.make_async_copy(line, bias_out, store_sem.at[2])
    bias_store.start()

    def end_sends(step):
        q_copy(step).wait_send()
        g_copy(step).wait_send()
        c_copy(step, enc).wait_send()
        dq_copy(step, enc).wait_send()
        c_copy(step, to_peer(step)).wait_recv()
        dq_copy(step, to_peer(step)).wait_recv()

    each(1, n_enc, end_sends)
    each(1, total, lambda step: b_copy(step, flat).wait_send())
    for copy in own:
        copy.wait()
    key_store.wait()
    value_store.wait()
    bias_store.wait()


def write_out(*refs):
    sources, targets, sem = refs[:5], refs[5:10], refs[10]
    copies = [
        pltpu.make_async_copy(source, target, sem.at[i])
        for i, (source, target) in enumerate(zip(sources, targets))
    ]
    for copy in copies:
        copy.start()
    for copy in copies:
        copy.wait()


def local(n_dp, n_seq, n_enc, queries, cotangent, key_pool, value_pool, counts, neighbour_ids, rel_bias):
    pool = key_pool.shape[2]
    tokens = pool * PASSAGE
    slots = neighbour_ids.shape[-1]
    table = rel_bias.shape[1]
    total = n_dp * n_seq
    all_rows = n_enc * ROWS
    batch_rows = ROWS * (2 if n_enc % 2 == 0 else 1)
    anywhere = pl.BlockSpec(memory_space=pl.ANY)
    held = pl.BlockSpec(memory_space=pltpu.HBM)
    results = pl.pallas_call(
        functools.partial(kernel, n_dp, n_seq, n_enc, pool, slots),
        out_shape=[
            jax.ShapeDtypeStruct(queries.shape, BF16),
            jax.ShapeDtypeStruct(queries.shape, BF16),
            jax.ShapeDtypeStruct((tokens, HEAD_DIM), BF16),
            jax.ShapeDtypeStruct((tokens, HEAD_DIM), BF16),
            jax.ShapeDtypeStruct(rel_bias.shape, F32),
        ],
        in_specs=[held] * 7,
        out_specs=[anywhere] * 5,
        scratch_shapes=[
            pltpu.VMEM((all_rows, HEAD_DIM), BF16),
            pltpu.VMEM((all_rows, HEAD_DIM), BF16),
            pltpu.VMEM((tokens, HEAD_DIM), BF16),
            pltpu.VMEM((tokens, HEAD_DIM), BF16),
            pltpu.VMEM((HEAD_DIM, tokens), BF16),
            pltpu.VMEM((HEAD_DIM, tokens), BF16),
            pltpu.SMEM(counts.shape[::-1], jnp.int32),
            pltpu.SMEM(neighbour_ids.shape, jnp.int32),
            pltpu.VMEM((1, table), F32),
            pltpu.VMEM((1, WIDE), F32),
            pltpu.VMEM((PASSAGE, batch_rows), F32),
            pltpu.VMEM((tokens, batch_rows), F32),
            pltpu.VMEM((tokens, batch_rows), F32),
            pltpu.VMEM((tokens, all_rows), BF16),
            pltpu.VMEM((tokens, all_rows), BF16),
            pltpu.VMEM((PASSAGE, batch_rows), F32),
            pltpu.VMEM((all_rows, HEAD_DIM), BF16),
            pltpu.VMEM((all_rows, HEAD_DIM), BF16),
            pltpu.VMEM((tokens, HEAD_DIM), BF16),
            pltpu.VMEM((tokens, HEAD_DIM), BF16),
            pltpu.VMEM((total, 1, WIDE), F32),
            pltpu.VMEM((1, WIDE), F32),
            pltpu.SemaphoreType.DMA((7,)),
            pltpu.SemaphoreType.DMA((2,)),
            pltpu.SemaphoreType.DMA((3,)),
        ]
        + [pltpu.SemaphoreType.DMA((n_enc,))] * 8
        + [pltpu.SemaphoreType.DMA((total,))] * 2,
        compiler_params=pltpu.CompilerParams(
            collective_id=0, has_side_effects=True, vmem_limit_bytes=48 * 1024 * 1024
        ),
        name="retrieval_attention",
    )(
        pltpu.with_memory_space_constraint(queries, pltpu.HBM),
        pltpu.with_memory_space_constraint(cotangent, pltpu.HBM),
        pltpu.with_memory_space_constraint(key_pool.reshape(tokens, HEAD_DIM), pltpu.HBM),
        pltpu.with_memory_space_constraint(value_pool.reshape(tokens, HEAD_DIM), pltpu.HBM),
        pltpu.with_memory_space_constraint(counts.T, pltpu.HBM),
        pltpu.with_memory_space_constraint(neighbour_ids, pltpu.HBM),
        pltpu.with_memory_space_constraint(rel_bias, pltpu.HBM),
    )
    context, query_grad, key_grad, value_grad, bias_grad = pl.pallas_call(
        write_out,
        out_shape=[jax.ShapeDtypeStruct(x.shape, x.dtype) for x in results],
        in_specs=[anywhere] * 5,
        out_specs=[held] * 5,
        scratch_shapes=[pltpu.SemaphoreType.DMA((5,))],
        compiler_params=pltpu.CompilerParams(vmem_limit_bytes=2 * 1024 * 1024),
        name="write_out",
    )(*results)
    return (
        context,
        query_grad,
        key_grad.reshape(key_pool.shape),
        value_grad.reshape(value_pool.shape),
        bias_grad,
    )


def solution(mesh):
    in_specs = (
        P(("dp", "enc"), "seq", None),
        P(("dp", "enc"), "seq", None),
        P("dp", "seq", None, None, "enc"),
        P("dp", "seq", None, None, "enc"),
        P("dp", "seq"),
        P("dp", "seq", None),
        P("enc", None),
    )
    out_specs = (
        P(("dp", "enc"), "seq", None),
        P(("dp", "enc"), "seq", None),
        P("dp", "seq", None, None, "enc"),
        P("dp", "seq", None, None, "enc"),
        P("enc", None),
    )
    body = functools.partial(local, mesh.shape["dp"], mesh.shape["seq"], mesh.shape["enc"])
    return jax.shard_map(body, mesh=mesh, in_specs=in_specs, out_specs=out_specs, check_vma=False)
```
